256 devices in a mesh: row: 32 (over x, y, core), col: 8 (over z).
Axes of the slice: x: 4, y: 4, z: 8, core: 2. Of those that a mesh axis runs over, the one named last changes fastest.
Arguments:
- data_slab: float32 [24576, 32768], P('row', 'col'), may hold values from -4.8 to 4.8
- sketch: float32 [32768, 64], P('col'), may hold values from -0.03125 to 0.03125
Outputs:
- range_basis: float32 [24576, 64], P('row')
- projected: float32 [64, 32768], P(None, 'col')
The draws below stay inside these ranges and needn't reach their ends.
All inputs are finite; a program needn't handle non-finite values.
Results may differ from the reference program's by a relative error of at most 0.0003.
Values sent between devices are 32-bit elements; how exact they have to be, the bound alone decides.
No kernel may reach another device: no remote copies, remote signals or barrier semaphores. Data moves between devices by JAX's collectives and lax.ppermute only.
A program may use at most 64 MiB of HBM per device.

```python
import math
import jax
import jax.numpy as jnp
from jax import lax

K = 64
NV = 32768
ROWS = 24576


def draw_data_slab(key, part):
    key = jax.random.fold_in(key, 11)
    key_list = jax.random.split(key, 5)
    positions = jnp.arange(ROWS, dtype=jnp.float32)[:, None] / ROWS
    rough_part = jnp.clip(jax.random.normal(key_list[0], (ROWS, NV), jnp.float32), -4.0, 4.0)
    row_scale = jnp.exp(jax.random.uniform(key_list[1], (ROWS, 1), jnp.float32, math.log(0.1), 0.0))
    mix_weight = jnp.clip(jax.random.normal(key_list[2], (ROWS, 1), jnp.float32), -2.0, 2.0)
    common_row = jnp.clip(jax.random.normal(key_list[3], (1, NV), jnp.float32), -2.0, 2.0)
    row_trend = 1.0 + 2.0 * positions
    col_scale = jnp.exp(jax.random.uniform(key_list[4], (1, NV), jnp.float32, math.log(0.1), 0.0))
    return 0.1 * row_trend * row_scale * col_scale * (rough_part + mix_weight * common_row)


def levels(key, extent, shards, smallest, largest):
    def one(position, shards_of):
        steps = jax.random.uniform(jax.random.fold_in(jax.random.fold_in(key, 6), position), (shards_of,), jnp.float32, smallest / len(shards), largest / len(shards))
        return jnp.repeat(jnp.exp(steps), extent[position] // shards_of).reshape((-1,) + (1,) * (len(extent) - position - 1))

    level = one(*shards[0])
    for cut in shards[1:]:
        level = level * one(*cut)
    return level


def bell_draw(rng, dims, deviation, limit, cuts=(), kind=jnp.bfloat16):
    level = levels(rng, dims, cuts, -0.22, 0.18) if cuts else 1.0
    result = jax.random.normal(rng, dims, jnp.float32) * deviation * level
    return jnp.minimum(jnp.maximum(result, -limit), limit).astype(kind)


def setup_inputs(seed: int = 0) -> dict:
    arg_keys = jax.random.split(jax.random.key(seed), 3)
    return {
        "data_slab": draw_data_slab(jax.random.fold_in(arg_keys[2], 71), 0),
        "sketch": bell_draw(arg_keys[1], (NV, K), NV ** -0.5, 0.03125, ((0, 8),), jnp.float32),
    }


def reference(data_slab, sketch):
    sample = jnp.dot(data_slab.astype(jnp.float32), sketch.astype(jnp.float32), precision=lax.Precision.HIGHEST, preferred_element_type=jnp.float32)
    factor_q, factor_r = jnp.linalg.qr(sample)
    diag_signs = jnp.sign(jnp.diagonal(factor_r))
    basis_q = factor_q * diag_signs[None, :]
    projected = jnp.dot(basis_q.T.astype(jnp.float32), data_slab.astype(jnp.float32), precision=lax.Precision.HIGHEST, preferred_element_type=jnp.float32)
    range_basis = basis_q * math.sqrt(ROWS)
    return (range_basis, projected)
```

```python
import functools
import math

import jax
import jax.numpy as jnp
from jax import lax
from jax.experimental import pallas as pl
from jax.experimental.pallas import tpu as pltpu
from jax.sharding import PartitionSpec as P

F32 = jnp.float32
BF16 = jnp.bfloat16
VMEM = pltpu.VMEM
K = 64
LANES = 128
QUARTERS = 4
BLOCKS = 32
GROUPS = 8
PER_GROUP = 4


def split(value):
    high = value.astype(BF16)
    return high, (value - high.astype(F32)).astype(BF16)


def own_quarter():
    z = lax.axis_index("col")
    return jnp.where(z < QUARTERS, z, 2 * QUARTERS - 1 - z)


def position():
    row = lax.axis_index("row")
    core, y, x = row % 2, (row // 2) % 4, row // 8
    return core, jnp.where(core == 0, x, y), jnp.where(core == 0, y, x)


def group_place(group):
    core, first, second = position()
    if group < PER_GROUP:
        return core * PER_GROUP + (first ^ group), second
    return (1 - core) * PER_GROUP + (second ^ (group - PER_GROUP)), first


def sample_kernel(data_ref, sketch_ref, *refs):
    outs, (data, sketch, weights, sems) = refs[:QUARTERS], refs[QUARTERS:]
    rows = data.shape[1]
    mine = own_quarter()
    load = pltpu.make_async_copy(sketch_ref, sketch, sems.at[QUARTERS])
    load.start()
    order = (3, 2, 1, 0)
    copies = {}
    for j in order:
        start = pl.multiple_of((mine ^ j) * rows, rows)
        copies[j] = pltpu.make_async_copy(data_ref.at[pl.ds(start, rows)], data.at[j], sems.at[j])
        copies[j].start()
    load.wait()
    high, low = split(sketch[...])
    weights[...] = jnp.concatenate([high, low], axis=1)
    lane = lax.broadcasted_iota(jnp.int32, (rows // 2, LANES), 1)
    for j in order:
        copies[j].wait()
        high, low = split(data[j])
        total = jnp.dot(high, weights[...], preferred_element_type=F32)
        total += jnp.dot(low, weights[...], preferred_element_type=F32)
        total += pltpu.roll(total, K, axis=1)
        outs[j][...] = jnp.where(lane < K, total[: rows // 2], total[rows // 2 :])


def partial_sample(data_slab, sketch):
    rows, columns = data_slab.shape
    quarter = rows // QUARTERS
    return pl.pallas_call(
        sample_kernel,
        out_shape=[jax.ShapeDtypeStruct((quarter // 2, LANES), F32)] * QUARTERS,
        in_specs=[pl.BlockSpec(memory_space=pl.ANY)] * 2,
        out_specs=[pl.BlockSpec(memory_space=VMEM)] * QUARTERS,
        scratch_shapes=[
            VMEM((QUARTERS, quarter, columns), F32),
            VMEM((columns, K), F32),
            VMEM((columns, LANES), BF16),
            pltpu.SemaphoreType.DMA((QUARTERS + 1,)),
        ],
        compiler_params=pltpu.CompilerParams(vmem_limit_bytes=40 * 2**20),
        cost_estimate=pl.CostEstimate(flops=8 * rows * columns * K, bytes_accessed=4 * rows * columns, transcendentals=0),
    )(data_slab, sketch)


def term_kernel(s0, s1, s2, s3, data_ref, keep_ref, send_ref, data, sample, sems):
    groups, rows, width = data.shape
    quarter = rows // QUARTERS
    half = quarter // 2
    mine = own_quarter()
    order = (4, 5, 6, 7, 0, 1, 2, 3)
    copies = {}
    for g in order:
        place, _ = group_place(g)
        start = pl.multiple_of(place * width, width)
        copies[g] = pltpu.make_async_copy(data_ref.at[:, pl.ds(start, width)], data.at[g], sems.at[g])
        copies[g].start()
    for j, ref in enumerate((s0, s1, s2, s3)):
        start = pl.multiple_of((mine ^ j) * quarter, quarter)
        sample[pl.ds(start, half), :] = ref[:, :K]
        sample[pl.ds(start + half, half), :] = ref[:, K:]
    high, low = split(sample[...].T)
    left = jnp.concatenate([high, low], axis=0)
    gram = lax.dot_general(left, left, (((1,), (1,)), ((), ())), preferred_element_type=F32)
    gram = gram[:K] + gram[K:]
    gram = gram + pltpu.roll(gram, K, axis=1)
    keep_ref[BLOCKS // 2] = gram
    send_ref[BLOCKS // 2] = gram
    for g in order:
        copies[g].wait()
        _, mask = group_place(g)
        high, low = split(data[g])
        total = jnp.dot(left, high, preferred_element_type=F32)
        total += jnp.dot(left, low, preferred_element_type=F32)
        total = total[:K] + total[K:]
        out_ref, base = (keep_ref, g * PER_GROUP) if g < PER_GROUP else (send_ref, (g - PER_GROUP) * PER_GROUP)
        for t in range(PER_GROUP):
            out_ref[base + (mask ^ t)] = total[:, t * LANES : (t + 1) * LANES]


def partial_terms(quarters, data_slab):
    rows, columns = data_slab.shape
    width = columns // GROUPS
    return pl.pallas_call(
        term_kernel,
        out_shape=[jax.ShapeDtypeStruct((BLOCKS // 2 + 1, K, LANES), F32)] * 2,
        in_specs=[pl.BlockSpec(memory_space=VMEM)] * QUARTERS + [pl.BlockSpec(memory_space=pl.ANY)],
        out_specs=[pl.BlockSpec(memory_space=VMEM)] * 2,
        scratch_shapes=[
            VMEM((GROUPS, rows, width), F32),
            VMEM((rows, K), F32),
            pltpu.SemaphoreType.DMA((GROUPS,)),
        ],
        compiler_params=pltpu.CompilerParams(vmem_limit_bytes=40 * 2**20),
        cost_estimate=pl.CostEstimate(flops=8 * rows * columns * K, bytes_accessed=4 * rows * columns, transcendentals=0),
    )(*quarters, data_slab)


def basis_kernel(scale, gram_ref, s0, s1, s2, s3, inverse_ref, basis_ref):
    lane = lax.broadcasted_iota(jnp.int32, (K, LANES), 1)
    row = lax.broadcasted_iota(jnp.int32, (K, LANES), 0)
    work = jnp.where(lane < K, gram_ref[...], jnp.where(lane == row + K, 1.0, 0.0))
    parts = [work[8 * i : 8 * i + 8] for i in range(K // 8)]
    sub = lax.broadcasted_iota(jnp.int32, (8, 1), 0)
    pivots = []
    for j in range(K):
        block, at = divmod(j, 8)
        line = parts[block][at : at + 1]
        pivot = line[:, j : j + 1]
        pivots.append(pivot)
        scaled = line * (1.0 / pivot)
        for i in range(block, K // 8):
            factor = parts[i][:, j : j + 1]
            if i == block:
                factor = jnp.where(sub > at, factor, 0.0)
            parts[i] = parts[i] - factor * scaled
    for i in range(K // 8):
        diagonal = jnp.concatenate(pivots[8 * i : 8 * i + 8], axis=0)
        parts[i] = parts[i] * (1.0 / jnp.sqrt(diagonal))
    inverse = jnp.concatenate(parts, axis=0)[:, K:]
    inverse_ref[...] = inverse
    mine = own_quarter()
    half = s0.shape[0]
    for j, ref in enumerate((s0, s1, s2, s3)):
        start = pl.multiple_of((mine ^ j) * 2 * half, 2 * half)
        for side in range(2):
            product = lax.dot_general(
                ref[:, side * K : (side + 1) * K],
                inverse * scale,
                (((1,), (1,)), ((), ())),
                precision=lax.Precision.HIGHEST,
                preferred_element_type=F32,
            )
            basis_ref[pl.ds(start + side * half, half), :] = product


def basis_of(gram, quarters, rows, scale):
    return pl.pallas_call(
        functools.partial(basis_kernel, scale),
        out_shape=[jax.ShapeDtypeStruct((K, K), F32), jax.ShapeDtypeStruct((rows, K), F32)],
        in_specs=[pl.BlockSpec(memory_space=VMEM)] * (1 + QUARTERS),
        out_specs=[pl.BlockSpec(memory_space=VMEM)] * 2,
        cost_estimate=pl.CostEstimate(flops=12 * rows * K * K, bytes_accessed=8 * rows * K, transcendentals=K),
    )(gram, *quarters)


def apply_kernel(inverse_ref, own_ref, other_ref, out_ref):
    high, low = split(inverse_ref[...])
    left = jnp.concatenate([high, low, high], axis=1)
    width = PER_GROUP * LANES
    for g in range(GROUPS):
        ref = own_ref if g < PER_GROUP else other_ref
        base = (g % PER_GROUP) * PER_GROUP
        place, mask = group_place(g)
        value = jnp.concatenate([ref[base + t] for t in range(PER_GROUP)], axis=1)
        high, low = split(value)
        right = jnp.concatenate([high, high, low], axis=0)
        total = jnp.dot(left, right, preferred_element_type=F32)
        for t in range(PER_GROUP):
            start = pl.multiple_of(place * width + (mask ^ t) * LANES, LANES)
            out_ref[:, pl.ds(start, LANES)] = total[:, t * LANES : (t + 1) * LANES]


def applied(inverse, own, other):
    columns = BLOCKS * LANES
    return pl.pallas_call(
        apply_kernel,
        out_shape=jax.ShapeDtypeStruct((K, columns), F32),
        in_specs=[pl.BlockSpec(memory_space=VMEM)] * 3,
        out_specs=pl.BlockSpec(memory_space=VMEM),
        cost_estimate=pl.CostEstimate(flops=6 * columns * K * K, bytes_accessed=8 * columns * K, transcendentals=0),
    )(inverse, own, other)


def along_col(value, mask):
    return lax.ppermute(value, "col", [(i, i ^ mask) for i in range(8)])


def along_row(value, masks):
    return lax.ppermute(value, "row", [(i, i ^ masks[i % 2]) for i in range(32)])


CORE = (1, 1)
FIRST = [(t << 3, t << 1) for t in range(4)]
SECOND = [(t << 1, t << 3) for t in range(4)]


def body(data_slab, sketch):
    rows = data_slab.shape[0]
    parts = partial_sample(data_slab, sketch)
    owned = parts[0] + along_col(parts[1], 1) + along_col(parts[2], 2) + along_col(parts[3], 3)
    owned = owned + along_col(owned, 7)
    quarters = [owned] + [along_col(owned, t) for t in (1, 2, 3)]

    keep, send = partial_terms(quarters, data_slab)
    total = keep + along_row(send, CORE)
    gram = total[16:]
    got = [along_row(jnp.concatenate([total[4 * t : 4 * t + 4], gram]), FIRST[t]) for t in (1, 2, 3)]
    total = jnp.concatenate([total[:4], gram]) + got[0] + got[1] + got[2]
    gram = total[4:]
    got = [along_row(jnp.concatenate([total[t : t + 1], gram]), SECOND[t]) for t in (1, 2, 3)]
    total = jnp.concatenate([total[:1], gram]) + got[0] + got[1] + got[2]

    inverse, range_basis = basis_of(total[1], quarters, rows, math.sqrt(rows * lax.axis_size("row")))

    block = total[:1]
    row_of = jnp.concatenate([block] + [along_row(block, SECOND[t]) for t in (1, 2, 3)])
    own = jnp.concatenate([row_of] + [along_row(row_of, FIRST[t]) for t in (1, 2, 3)])
    other = along_row(own, CORE)
    return range_basis, applied(inverse, own, other)


def solution(mesh):
    placed = (P("row", "col"), P("col", None))
    return jax.shard_map(
        body,
        mesh=mesh,
        in_specs=placed,
        out_specs=(P("row", None), P(None, "col")),
        check_vma=False,
    )
```

```python
import functools
import math

import jax
import jax.numpy as jnp
from jax import lax
from jax.experimental import pallas as pl
from jax.experimental.pallas import tpu as pltpu
from jax.sharding import PartitionSpec as P

F32 = jnp.float32
BF16 = jnp.bfloat16
VMEM = pltpu.VMEM
MIB = 2**20
K = 64
LANES = 128
HALVES = 2
CHUNKS = 4
BLOCKS = 32
GROUPS = 8
PER_GROUP = 4


def split(value):
    high = value.astype(BF16)
    return high, (value - high.astype(F32)).astype(BF16)


def own_half():
    z = lax.axis_index("col")
    return jnp.where(z < 4, z, 7 - z) % HALVES


def position():
    row = lax.axis_index("row")
    core, y, x = row % 2, (row // 2) % 4, row // 8
    return core, jnp.where(core == 0, x, y), jnp.where(core == 0, y, x)


def group_place(group):
    core, first, second = position()
    if group < PER_GROUP:
        return core * PER_GROUP + (first ^ group)
    return (1 - core) * PER_GROUP + (second ^ (group - PER_GROUP))


def vmem(count):
    return [pl.BlockSpec(memory_space=VMEM)] * count


def packed(value):
    half = value.shape[0] // 2
    return jnp.concatenate([value[:half], value[half:]], axis=1)


def unpacked(value):
    return jnp.concatenate([value[:, :K], value[:, K:]], axis=0)


def sample_half(data_ref, half, weights, out_ref, terms_ref, data, sems, prepare):
    count, chunk = data.shape[:2]
    rows = count * chunk
    copies = []
    for i in range(count):
        start = pl.multiple_of(half * rows + i * chunk, chunk)
        copies.append(pltpu.make_async_copy(data_ref.at[pl.ds(start, chunk)], data.at[i], sems.at[i]))
        copies[i].start()
    prepare()
    lane = lax.broadcasted_iota(jnp.int32, (chunk, LANES), 1)
    totals = []
    for i in range(count):
        copies[i].wait()
        high, low = split(data[i])
        terms_ref[pl.ds(i * chunk, chunk), :] = high
        terms_ref[pl.ds(rows + i * chunk, chunk), :] = low
        total = jnp.dot(high, weights[...], preferred_element_type=F32)
        total += jnp.dot(low, weights[...], preferred_element_type=F32)
        totals.append(total + pltpu.roll(total, K, axis=1))
    for i in range(count // 2):
        out_ref[pl.ds(i * chunk, chunk), :] = jnp.where(lane < K, totals[i], totals[i + count // 2])


def send_kernel(data_ref, sketch_ref, out_ref, terms_ref, weights_ref, data, sketch, sems):
    load = pltpu.make_async_copy(sketch_ref, sketch, sems.at[CHUNKS])
    load.start()

    def prepare():
        load.wait()
        high, low = split(sketch[...].T)
        weights_ref[...] = jnp.concatenate([high, low], axis=1)

    sample_half(data_ref, 1 - own_half(), weights_ref, out_ref, terms_ref, data, sems, prepare)


def keep_kernel(data_ref, weights_ref, out_ref, terms_ref, data, sems):
    sample_half(data_ref, own_half(), weights_ref, out_ref, terms_ref, data, sems, lambda: None)


def partial_samples(data_slab, sketch_t):
    rows, columns = data_slab.shape
    half = rows // HALVES
    chunk = half // CHUNKS
    cost = pl.CostEstimate(flops=4 * rows * columns * K, bytes_accessed=4 * half * columns, transcendentals=0)
    outs = [jax.ShapeDtypeStruct((half // 2, LANES), F32), jax.ShapeDtypeStruct((2 * half, columns), BF16)]
    sent, sent_terms, weights = pl.pallas_call(
        send_kernel,
        out_shape=outs + [jax.ShapeDtypeStruct((columns, LANES), BF16)],
        in_specs=[pl.BlockSpec(memory_space=pl.ANY)] * 2,
        out_specs=vmem(3),
        scratch_shapes=[
            VMEM((CHUNKS, chunk, columns), F32),
            VMEM((K, columns), F32),
            pltpu.SemaphoreType.DMA((CHUNKS + 1,)),
        ],
        compiler_params=pltpu.CompilerParams(vmem_limit_bytes=44 * MIB),
        cost_estimate=cost,
    )(data_slab, sketch_t)
    kept, kept_terms = pl.pallas_call(
        keep_kernel,
        out_shape=outs,
        in_specs=[pl.BlockSpec(memory_space=pl.ANY)] + vmem(1),
        out_specs=vmem(2),
        scratch_shapes=[VMEM((CHUNKS, chunk, columns), F32), pltpu.SemaphoreType.DMA((CHUNKS,))],
        compiler_params=pltpu.CompilerParams(vmem_limit_bytes=40 * MIB),
        cost_estimate=cost,
    )(data_slab, weights)
    return sent, sent_terms, kept, kept_terms


def left_of(sample):
    high, low = split(unpacked(sample).T)
    left = jnp.concatenate([high, low], axis=0)
    return left, jnp.concatenate([left, left], axis=1)


def first_term_kernel(sample_ref, terms_ref, out_ref):
    _, left = left_of(sample_ref[...])
    width = out_ref.shape[1] // GROUPS
    for g in range(GROUPS):
        at = pl.ds(g * width, width)
        total = jnp.dot(left, terms_ref[:, at], preferred_element_type=F32)
        out_ref[:, at] = total[:K] + total[K:]


def second_term_kernel(other_ref, sample_ref, terms_ref, begun_ref, keep_ref, send_ref):
    single, left = left_of(sample_ref[...])
    other, _ = left_of(other_ref[...])
    both = jnp.concatenate([single, other], axis=1)
    gram = lax.dot_general(both, both, (((1,), (1,)), ((), ())), preferred_element_type=F32)
    gram = gram[:K] + gram[K:]
    gram = gram + pltpu.roll(gram, K, axis=1)
    keep_ref[BLOCKS // 2] = gram
    send_ref[BLOCKS // 2] = gram
    width = PER_GROUP * LANES
    for g in (4, 5, 6, 7, 0, 1, 2, 3):
        at = pl.ds(pl.multiple_of(group_place(g) * width, width), width)
        total = jnp.dot(left, terms_ref[:, at], preferred_element_type=F32)
        total = total[:K] + total[K:] + begun_ref[:, at]
        out_ref, base = (keep_ref, g) if g < PER_GROUP else (send_ref, g - PER_GROUP)
        for t in range(PER_GROUP):
            out_ref[base * PER_GROUP + t] = total[:, t * LANES : (t + 1) * LANES]


def term_cost(terms):
    return pl.CostEstimate(flops=4 * K * terms.size, bytes_accessed=2 * terms.size, transcendentals=0)


def first_terms(sample, terms):
    return pl.pallas_call(
        first_term_kernel,
        out_shape=jax.ShapeDtypeStruct((K, terms.shape[1]), F32),
        in_specs=vmem(2),
        out_specs=vmem(1)[0],
        compiler_params=pltpu.CompilerParams(vmem_limit_bytes=16 * MIB),
        cost_estimate=term_cost(terms),
    )(sample, terms)


def second_terms(other, sample, terms, begun):
    return pl.pallas_call(
        second_term_kernel,
        out_shape=[jax.ShapeDtypeStruct((BLOCKS // 2 + 1, K, LANES), F32)] * 2,
        in_specs=vmem(4),
        out_specs=vmem(2),
        compiler_params=pltpu.CompilerParams(vmem_limit_bytes=16 * MIB),
        cost_estimate=term_cost(terms),
    )(other, sample, terms, begun)


def inverse_kernel(gram_ref, inverse_ref):
    lane = lax.broadcasted_iota(jnp.int32, (K, LANES), 1)
    row = lax.broadcasted_iota(jnp.int32, (K, LANES), 0)
    work = jnp.where(lane < K, gram_ref[...], jnp.where(lane == row + K, 1.0, 0.0))
    parts = [work[8 * i : 8 * i + 8] for i in range(K // 8)]
    sub = lax.broadcasted_iota(jnp.int32, (8, 1), 0)
    pivots = []
    for j in range(K):
        block, at = divmod(j, 8)
        line = parts[block][at : at + 1]
        pivot = line[:, j : j + 1]
        pivots.append(pivot)
        scaled = line * (1.0 / pivot)
        for i in range(block, K // 8):
            factor = parts[i][:, j : j + 1]
            if i == block:
                factor = jnp.where(sub > at, factor, 0.0)
            parts[i] = parts[i] - factor * scaled
    for i in range(K // 8):
        diagonal = jnp.concatenate(pivots[8 * i : 8 * i + 8], axis=0)
        parts[i] = parts[i] * (1.0 / jnp.sqrt(diagonal))
    inverse_ref[...] = jnp.concatenate(parts, axis=0)[:, K:]


def inverse_of(gram):
    return pl.pallas_call(
        inverse_kernel,
        out_shape=jax.ShapeDtypeStruct((K, K), F32),
        in_specs=vmem(1),
        out_specs=vmem(1)[0],
        compiler_params=pltpu.CompilerParams(vmem_limit_bytes=8 * MIB),
        cost_estimate=pl.CostEstimate(flops=K**3 * 100, bytes_accessed=8 * K * K, transcendentals=K),
    )(gram)


def basis_kernel(scale, inverse_ref, own_ref, other_ref, basis_ref):
    half = basis_ref.shape[1] // HALVES
    left = inverse_ref[...] * scale
    own, other = [
        lax.dot_general(
            left,
            unpacked(ref[...]),
            (((1,), (1,)), ((), ())),
            precision=lax.Precision.HIGHEST,
            preferred_element_type=F32,
        )
        for ref in (own_ref, other_ref)
    ]
    is_first = own_half() == 0
    basis_ref[:, :half] = jnp.where(is_first, own, other)
    basis_ref[:, half:] = jnp.where(is_first, other, own)


def basis_of(inverse, own, other, rows, scale):
    return pl.pallas_call(
        functools.partial(basis_kernel, scale),
        out_shape=jax.ShapeDtypeStruct((K, rows), F32),
        in_specs=vmem(3),
        out_specs=vmem(1)[0],
        compiler_params=pltpu.CompilerParams(vmem_limit_bytes=8 * MIB),
        cost_estimate=pl.CostEstimate(flops=12 * rows * K * K, bytes_accessed=8 * rows * K, transcendentals=0),
    )(inverse, own, other)


def apply_kernel(inverse_ref, own_ref, other_ref, out_ref):
    high, low = split(inverse_ref[...])
    left = jnp.concatenate([high, low, high], axis=1)
    width = PER_GROUP * LANES
    for g in range(GROUPS):
        ref, base = (own_ref, g) if g < PER_GROUP else (other_ref, g - PER_GROUP)
        value = jnp.concatenate([ref[base * PER_GROUP + t] for t in range(PER_GROUP)], axis=1)
        high, low = split(value)
        right = jnp.concatenate([high, high, low], axis=0)
        at = pl.ds(pl.multiple_of(group_place(g) * width, width), width)
        out_ref[:, at] = jnp.dot(left, right, preferred_element_type=F32)


def applied(inverse, own, other):
    columns = BLOCKS * LANES
    return pl.pallas_call(
        apply_kernel,
        out_shape=jax.ShapeDtypeStruct((K, columns), F32),
        in_specs=vmem(3),
        out_specs=vmem(1)[0],
        compiler_params=pltpu.CompilerParams(vmem_limit_bytes=8 * MIB),
        cost_estimate=pl.CostEstimate(flops=6 * columns * K * K, bytes_accessed=8 * columns * K, transcendentals=0),
    )(inverse, own, other)


def along_col(value, mask):
    return lax.ppermute(value, "col", [(i, i ^ mask) for i in range(8)])


def along_row(value, masks):
    return lax.ppermute(value, "row", [(i, i ^ masks[i % 2]) for i in range(32)])


CORE = (1, 1)
FIRST = [(t << 3, t << 1) for t in range(4)]
SECOND = [(t << 1, t << 3) for t in range(4)]


def body(data_slab, sketch):
    rows = data_slab.shape[0]
    sent, sent_terms, kept, kept_terms = partial_samples(data_slab, sketch.T)
    own = kept + along_col(sent, 1)
    own = own + along_col(own, 2)
    own = own + along_col(own, 7)
    other = along_col(own, 1)

    begun = first_terms(own, kept_terms)
    keep, send = second_terms(own, other, sent_terms, begun)
    total = keep + along_row(send, CORE)
    gram = total[16:]
    got = [along_row(jnp.concatenate([total[4 * t : 4 * t + 4], gram]), FIRST[t]) for t in (1, 2, 3)]
    total = jnp.concatenate([total[:4], gram]) + got[0] + got[1] + got[2]
    got = [along_row(total, SECOND[t]) for t in (1, 2, 3)]
    total = total + got[0] + got[1] + got[2]

    inverse = inverse_of(total[4])
    block = total[:4]
    mine = jnp.concatenate([block] + [along_row(block, FIRST[t]) for t in (1, 2, 3)])
    mine, inverse = lax.optimization_barrier((mine, inverse))
    theirs = along_row(mine, CORE)
    range_basis = basis_of(inverse, own, other, rows, math.sqrt(rows * lax.axis_size("row")))
    return range_basis.T, applied(inverse, mine, theirs)


def solution(mesh):
    placed = (P("row", "col"), P("col", None))
    return jax.shard_map(
        body,
        mesh=mesh,
        in_specs=placed,
        out_specs=(P("row", None), P(None, "col")),
        check_vma=False,
    )
```

```python
import functools
import math

import jax
import jax.numpy as jnp
from jax import lax
from jax.experimental import pallas as pl
from jax.experimental.pallas import tpu as pltpu
from jax.sharding import PartitionSpec as P

F32 = jnp.float32
BF16 = jnp.bfloat16
VMEM = pltpu.VMEM
MIB = 2**20
K = 64
LANES = 128
QUARTERS = 4
CHUNKS = 2
BLOCKS = 32
GROUPS = 8
PER_GROUP = 4


def split(value):
    high = value.astype(BF16)
    return high, (value - high.astype(F32)).astype(BF16)


def own_quarter():
    z = lax.axis_index("col")
    return jnp.where(z < QUARTERS, z, 2 * QUARTERS - 1 - z)


def position():
    row = lax.axis_index("row")
    core, y, x = row % 2, (row // 2) % 4, row // 8
    return core, jnp.where(core == 0, x, y), jnp.where(core == 0, y, x)


def group_place(group):
    core, first, second = position()
    if group < PER_GROUP:
        return core * PER_GROUP + (first ^ group)
    return (1 - core) * PER_GROUP + (second ^ (group - PER_GROUP))


def vmem(count):
    return [pl.BlockSpec(memory_space=VMEM)] * count


def unpacked(value):
    return jnp.concatenate([value[:, :K], value[:, K:]], axis=0)


def sample_quarters(data_ref, masks, weights, outs, terms_ref, data, sems, prepare):
    chunk = data.shape[1]
    rows = CHUNKS * chunk
    mine = own_quarter()
    copies = []
    for i in range(len(masks) * CHUNKS):
        start = pl.multiple_of((mine ^ masks[i // CHUNKS]) * rows + i % CHUNKS * chunk, chunk)
        copies.append(pltpu.make_async_copy(data_ref.at[pl.ds(start, chunk)], data.at[i], sems.at[i]))
        copies[i].start()
    prepare()
    lane = lax.broadcasted_iota(jnp.int32, (chunk, LANES), 1)
    for q in range(len(masks)):
        totals = []
        for i in range(CHUNKS):
            at = q * CHUNKS + i
            copies[at].wait()
            high, low = split(data[at])
            terms_ref[pl.ds(2 * q * rows + i * chunk, chunk), :] = high
            terms_ref[pl.ds((2 * q + 1) * rows + i * chunk, chunk), :] = low
            total = jnp.dot(high, weights[...], preferred_element_type=F32)
            total += jnp.dot(low, weights[...], preferred_element_type=F32)
            totals.append(total + pltpu.roll(total, K, axis=1))
        outs[q][...] = jnp.where(lane < K, totals[0], totals[1])


SENT = (3, 2, 1)


def send_kernel(data_ref, sketch_ref, out3, out2, out1, terms_ref, weights_ref, data, sketch, sems):
    load = pltpu.make_async_copy(sketch_ref, sketch, sems.at[len(SENT) * CHUNKS])
    load.start()

    def prepare():
        load.wait()
        high, low = split(sketch[...].T)
        weights_ref[...] = jnp.concatenate([high, low], axis=1)

    sample_quarters(data_ref, SENT, weights_ref, (out3, out2, out1), terms_ref, data, sems, prepare)


def keep_kernel(data_ref, weights_ref, out_ref, terms_ref, data, sems):
    sample_quarters(data_ref, (0,), weights_ref, (out_ref,), terms_ref, data, sems, lambda: None)


def partial_samples(data_slab, sketch_t):
    rows, columns = data_slab.shape
    quarter = rows // QUARTERS
    chunk = quarter // CHUNKS
    sample = jax.ShapeDtypeStruct((chunk, LANES), F32)

    def cost(count):
        return pl.CostEstimate(
            flops=8 * count * quarter * columns * K, bytes_accessed=4 * count * quarter * columns, transcendentals=0
        )

    def scratch(count):
        return [VMEM((count * CHUNKS, chunk, columns), F32)]

    *sent, sent_terms, weights = pl.pallas_call(
        send_kernel,
        out_shape=[sample] * len(SENT)
        + [
            jax.ShapeDtypeStruct((2 * len(SENT) * quarter, columns), BF16),
            jax.ShapeDtypeStruct((columns, LANES), BF16),
        ],
        in_specs=[pl.BlockSpec(memory_space=pl.ANY)] * 2,
        out_specs=vmem(len(SENT) + 2),
        scratch_shapes=scratch(len(SENT))
        + [VMEM((K, columns), F32), pltpu.SemaphoreType.DMA((len(SENT) * CHUNKS + 1,))],
        compiler_params=pltpu.CompilerParams(vmem_limit_bytes=42 * MIB),
        cost_estimate=cost(len(SENT)),
    )(data_slab, sketch_t)
    kept, kept_terms = pl.pallas_call(
        keep_kernel,
        out_shape=[sample, jax.ShapeDtypeStruct((2 * quarter, columns), BF16)],
        in_specs=[pl.BlockSpec(memory_space=pl.ANY)] + vmem(1),
        out_specs=vmem(2),
        scratch_shapes=scratch(1) + [pltpu.SemaphoreType.DMA((CHUNKS,))],
        compiler_params=pltpu.CompilerParams(vmem_limit_bytes=40 * MIB),
        cost_estimate=cost(1),
    )(data_slab, weights)
    return sent, sent_terms, kept, kept_terms


def left_of(sample):
    high, low = split(unpacked(sample).T)
    left = jnp.concatenate([high, low], axis=0)
    return left, jnp.concatenate([left, left], axis=1)


def first_term_kernel(own_ref, sample_ref, kept_ref, sent_ref, out_ref):
    _, left = left_of(own_ref[...])
    _, other = left_of(sample_ref[...])
    size = kept_ref.shape[0]
    width = out_ref.shape[1] // GROUPS
    for g in range(GROUPS):
        at = pl.ds(g * width, width)
        total = jnp.dot(left, kept_ref[:, at], preferred_element_type=F32)
        total += jnp.dot(other, sent_ref[:size, at], preferred_element_type=F32)
        out_ref[:, at] = total[:K] + total[K:]


def second_term_kernel(s0, s3, s2, s1, sent_ref, begun_ref, keep_ref, send_ref):
    singles, lefts = zip(*[left_of(ref[...]) for ref in (s2, s1, s0, s3)])
    left = jnp.concatenate(lefts[:2], axis=1)
    every = jnp.concatenate(singles, axis=1)
    gram = lax.dot_general(every, every, (((1,), (1,)), ((), ())), preferred_element_type=F32)
    gram = gram[:K] + gram[K:]
    gram = gram + pltpu.roll(gram, K, axis=1)
    lane = lax.broadcasted_iota(jnp.int32, (K // 2, LANES), 1)
    gram = jnp.where(lane < K, gram[: K // 2], gram[K // 2 :])
    keep_ref[BLOCKS // 2 * K :, :] = gram
    send_ref[BLOCKS // 2 * K :, :] = gram
    size = left.shape[1]
    width = PER_GROUP * LANES
    for g in (4, 5, 6, 7, 0, 1, 2, 3):
        at = pl.ds(pl.multiple_of(group_place(g) * width, width), width)
        total = jnp.dot(left, sent_ref[size // 2 :, at], preferred_element_type=F32)
        total = total[:K] + total[K:] + begun_ref[:, at]
        out_ref, base = (keep_ref, g) if g < PER_GROUP else (send_ref, g - PER_GROUP)
        for t in range(PER_GROUP):
            out_ref[pl.ds((base * PER_GROUP + t) * K, K), :] = total[:, t * LANES : (t + 1) * LANES]


def term_cost(rows, columns):
    return pl.CostEstimate(flops=8 * K * rows * columns, bytes_accessed=4 * rows * columns, transcendentals=0)


def first_terms(own, third, kept_terms, sent_terms):
    size, columns = kept_terms.shape
    return pl.pallas_call(
        first_term_kernel,
        out_shape=jax.ShapeDtypeStruct((K, columns), F32),
        in_specs=vmem(4),
        out_specs=vmem(1)[0],
        compiler_params=pltpu.CompilerParams(vmem_limit_bytes=16 * MIB),
        cost_estimate=term_cost(size, columns),
    )(own, third, kept_terms, sent_terms)


def second_terms(quarters, sent_terms, begun):
    size, columns = sent_terms.shape
    return pl.pallas_call(
        second_term_kernel,
        out_shape=[jax.ShapeDtypeStruct((BLOCKS // 2 * K + K // 2, LANES), F32)] * 2,
        in_specs=vmem(len(quarters) + 2),
        out_specs=vmem(2),
        compiler_params=pltpu.CompilerParams(vmem_limit_bytes=16 * MIB),
        cost_estimate=term_cost(size // 3, columns),
    )(*quarters, sent_terms, begun)


def inverse_kernel(gram_ref, inverse_ref):
    lane = lax.broadcasted_iota(jnp.int32, (K // 2, LANES), 1)
    row = lax.broadcasted_iota(jnp.int32, (K // 2, LANES), 0)
    upper = gram_ref[...]
    lower = pltpu.roll(upper, K, axis=1)
    work = jnp.concatenate(
        [
            jnp.where(lane < K, upper, jnp.where(lane == row + K, 1.0, 0.0)),
            jnp.where(lane < K, lower, jnp.where(lane == row + K + K // 2, 1.0, 0.0)),
        ],
        axis=0,
    )
    count = K // 8
    parts = [work[8 * i : 8 * i + 8] for i in range(count)]
    sub = lax.broadcasted_iota(jnp.int32, (8, LANES), 0)
    diagonal = [jnp.ones((8, LANES), F32)] * count

    def full(value):
        return jnp.broadcast_to(value, (8, LANES))

    for j in range(0, K, 4):
        block, at = divmod(j, 8)
        own = parts[block]
        c1, c2, c3, c4 = [[full(parts[i][:, j + c : j + c + 1]) for i in range(block, count)] for c in range(4)]
        r1, r2, r3, r4 = [full(own[at + r : at + r + 1]) for r in range(4)]
        a11, a12, a13, a14 = [full(c[0][at : at + 1]) for c in (c1, c2, c3, c4)]
        a22, a23, a24 = [full(c[0][at + 1 : at + 2]) for c in (c2, c3, c4)]
        a33, a34 = [full(c[0][at + 2 : at + 3]) for c in (c3, c4)]
        a44 = full(c4[0][at + 3 : at + 4])
        first = a11 * a22 - a12 * a12
        scale = 1.0 / first
        l31, l32 = (a22 * a13 - a12 * a23) * scale, (a11 * a23 - a12 * a13) * scale
        l41, l42 = (a22 * a14 - a12 * a24) * scale, (a11 * a24 - a12 * a14) * scale
        s33 = a33 - (l31 * a13 + l32 * a23)
        s34 = a34 - (l31 * a14 + l32 * a24)
        s44 = a44 - (l41 * a14 + l42 * a24)
        r3 = r3 - (l31 * r1 + l32 * r2)
        r4 = r4 - (l41 * r1 + l42 * r2)
        second = s33 * s44 - s34 * s34
        again = 1.0 / second
        v1, v2 = (a22 * r1 - a12 * r2) * scale, (a11 * r2 - a12 * r1) * scale
        v3, v4 = (s44 * r3 - s34 * r4) * again, (s33 * r4 - s34 * r3) * again
        p1, p3 = 1.0 / a11, 1.0 / s33
        rows = (r2 - a12 * p1 * r1, r3, r4 - s34 * p3 * r3)
        diag = (a11, first * p1, s33, second * p3)
        for r in range(4):
            diagonal[block] = jnp.where(sub == at + r, diag[r], diagonal[block])
        for i in range(block, count):
            f1, f2, f3, f4 = [c[i - block] for c in (c1, c2, c3, c4)]
            f3 = f3 - (f1 * l31 + f2 * l32)
            f4 = f4 - (f1 * l41 + f2 * l42)
            new = parts[i] - ((f1 * v1 + f2 * v2) + (f3 * v3 + f4 * v4))
            if i == block:
                new = jnp.where(sub > at + 3, new, own)
                for r in range(3):
                    new = jnp.where(sub == at + 1 + r, rows[r], new)
            parts[i] = new
    parts = [part * (1.0 / jnp.sqrt(diag)) for part, diag in zip(parts, diagonal)]
    inverse_ref[...] = jnp.concatenate(parts, axis=0)[:, K:]


def inverse_of(gram):
    return pl.pallas_call(
        inverse_kernel,
        out_shape=jax.ShapeDtypeStruct((K, K), F32),
        in_specs=vmem(1),
        out_specs=vmem(1)[0],
        compiler_params=pltpu.CompilerParams(vmem_limit_bytes=8 * MIB),
        cost_estimate=pl.CostEstimate(flops=K**3 * 100, bytes_accessed=8 * K * K, transcendentals=K),
    )(gram)


def basis_kernel(scale, inverse_ref, s0, s3, s2, s1, basis_ref, sample):
    half = s0.shape[0]
    mine = own_quarter()
    for mask, ref in ((0, s0), (3, s3), (2, s2), (1, s1)):
        start = pl.multiple_of((mine ^ mask) * 2 * half, 2 * half)
        sample[pl.ds(start, half), :] = ref[:, :K]
        sample[pl.ds(start + half, half), :] = ref[:, K:]
    basis_ref[...] = lax.dot_general(
        inverse_ref[...] * scale,
        sample[...],
        (((1,), (1,)), ((), ())),
        precision=lax.Precision.HIGHEST,
        preferred_element_type=F32,
    )


def basis_of(inverse, quarters, rows, scale):
    return pl.pallas_call(
        functools.partial(basis_kernel, scale),
        out_shape=jax.ShapeDtypeStruct((K, rows), F32),
        in_specs=vmem(1 + len(quarters)),
        out_specs=vmem(1)[0],
        scratch_shapes=[VMEM((rows, K), F32)],
        compiler_params=pltpu.CompilerParams(vmem_limit_bytes=8 * MIB),
        cost_estimate=pl.CostEstimate(flops=12 * rows * K * K, bytes_accessed=8 * rows * K, transcendentals=0),
    )(inverse, *quarters)


def apply_kernel(first_group, inverse_ref, value_ref, *refs):
    out_ref, parts, sems = refs[-3:]
    high, low = split(inverse_ref[...])
    left = jnp.concatenate([high, low, high], axis=1)
    width = PER_GROUP * LANES
    copies = []
    for g in range(PER_GROUP):
        rows = [value_ref[pl.ds((g * PER_GROUP + t) * K, K), :] for t in range(PER_GROUP)]
        high, low = split(jnp.concatenate(rows, axis=1))
        right = jnp.concatenate([high, high, low], axis=0)
        parts[g] = jnp.dot(left, right, preferred_element_type=F32)
        at = pl.ds(pl.multiple_of(group_place(first_group + g) * width, width), width)
        copies.append(pltpu.make_async_copy(parts.at[g], out_ref.at[:, at], sems.at[g]))
        copies[g].start()
    for copy in copies:
        copy.wait()


def applied(first_group, inverse, value, begun=None):
    columns = BLOCKS * LANES
    more = [] if begun is None else [begun]
    return pl.pallas_call(
        functools.partial(apply_kernel, first_group),
        out_shape=jax.ShapeDtypeStruct((K, columns), F32),
        in_specs=vmem(2) + [pl.BlockSpec(memory_space=pl.ANY)] * len(more),
        out_specs=pl.BlockSpec(memory_space=pl.ANY),
        input_output_aliases={2: 0} if more else {},
        scratch_shapes=[VMEM((PER_GROUP, K, PER_GROUP * LANES), F32), pltpu.SemaphoreType.DMA((PER_GROUP,))],
        compiler_params=pltpu.CompilerParams(vmem_limit_bytes=8 * MIB),
        cost_estimate=pl.CostEstimate(flops=3 * columns * K * K, bytes_accessed=4 * columns * K, transcendentals=0),
    )(inverse, value, *more)


def along_col(value, mask):
    return lax.ppermute(value, "col", [(i, i ^ mask) for i in range(8)])


def along_row(value, masks):
    return lax.ppermute(value, "row", [(i, i ^ masks[i % 2]) for i in range(32)])


CORE = (1, 1)
FIRST = [(t << 3, t << 1) for t in range(4)]
SECOND = [(t << 1, t << 3) for t in range(4)]


def body(data_slab, sketch):
    rows = data_slab.shape[0]
    sent, sent_terms, kept, kept_terms = partial_samples(data_slab, sketch.T)
    got = [along_col(part, mask) for part, mask in zip(sent, SENT)]
    own = kept + got[0] + got[1] + got[2]
    own = own + along_col(own, 7)
    quarters = [own] + [along_col(own, mask) for mask in SENT]

    begun = first_terms(own, quarters[1], kept_terms, sent_terms)
    keep, send = second_terms(quarters, sent_terms, begun)
    total = keep + along_row(send, CORE)
    size = PER_GROUP * K
    gram = total[4 * size :]
    got = [along_row(jnp.concatenate([total[t * size : (t + 1) * size], gram]), FIRST[t]) for t in (1, 2, 3)]
    total = jnp.concatenate([total[:size], gram]) + got[0] + got[1] + got[2]
    got = [along_row(total, SECOND[t]) for t in (1, 2, 3)]
    total = total + got[0] + got[1] + got[2]

    inverse = inverse_of(total[size:])
    block = total[:size]
    mine = jnp.concatenate([block] + [along_row(block, FIRST[t]) for t in (1, 2, 3)])
    range_basis = basis_of(inverse, quarters, rows, math.sqrt(rows * lax.axis_size("row")))
    mine, inverse, range_basis = lax.optimization_barrier((mine, inverse, range_basis))
    theirs = along_row(mine, CORE)
    projected = applied(PER_GROUP, inverse, theirs, applied(0, inverse, mine))
    return range_basis.T, projected


def solution(mesh):
    placed = (P("row", "col"), P("col", None))
    return jax.shard_map(
        body,
        mesh=mesh,
        in_specs=placed,
        out_specs=(P("row", None), P(None, "col")),
        check_vma=False,
    )
```

```python
import functools
import math

import jax
import jax.numpy as jnp
from jax import lax
from jax.experimental import pallas as pl
from jax.experimental.pallas import tpu as pltpu
from jax.sharding import PartitionSpec as P

F32 = jnp.float32
BF16 = jnp.bfloat16
VMEM = pltpu.VMEM
MIB = 2**20
K = 64
LANES = 128
QUARTERS = 4
CHUNKS = 2
BLOCKS = 32
GROUPS = 8
PER_GROUP = 4


def split(value):
    high = value.astype(BF16)
    return high, (value - high.astype(F32)).astype(BF16)


def own_quarter():
    z = lax.axis_index("col")
    return jnp.where(z < QUARTERS, z, 2 * QUARTERS - 1 - z)


def position():
    row = lax.axis_index("row")
    core, y, x = row % 2, (row // 2) % 4, row // 8
    return core, jnp.where(core == 0, x, y), jnp.where(core == 0, y, x)


def group_place(group):
    core, first, second = position()
    if group < PER_GROUP:
        return core * PER_GROUP + (first ^ group)
    return (1 - core) * PER_GROUP + (second ^ (group - PER_GROUP))


def in_hbm(value):
    return pltpu.with_memory_space_constraint(value, pltpu.HBM)


def vmem(count):
    return [pl.BlockSpec(memory_space=VMEM)] * count


def unpacked(value):
    return jnp.concatenate([value[:, :K], value[:, K:]], axis=0)


def sample_quarters(data_ref, masks, weights, outs, terms_ref, data, sems, prepare):
    chunk = data.shape[1]
    rows = CHUNKS * chunk
    mine = own_quarter()
    copies = []
    for i in range(len(masks) * CHUNKS):
        start = pl.multiple_of((mine ^ masks[i // CHUNKS]) * rows + i % CHUNKS * chunk, chunk)
        copies.append(pltpu.make_async_copy(data_ref.at[pl.ds(start, chunk)], data.at[i], sems.at[i]))
        copies[i].start()
    prepare()
    lane = lax.broadcasted_iota(jnp.int32, (chunk, LANES), 1)
    for q in range(len(masks)):
        totals = []
        for i in range(CHUNKS):
            at = q * CHUNKS + i
            copies[at].wait()
            high, low = split(data[at])
            terms_ref[pl.ds(2 * q * rows + i * chunk, chunk), :] = high
            terms_ref[pl.ds((2 * q + 1) * rows + i * chunk, chunk), :] = low
            total = jnp.dot(jnp.concatenate([high, low], axis=0), weights[...], preferred_element_type=F32)
            total = total[:chunk] + total[chunk:]
            totals.append(total + pltpu.roll(total, K, axis=1))
        half = CHUNKS // 2
        for i in range(half):
            outs[q][pl.ds(i * chunk, chunk), :] = jnp.where(lane < K, totals[i], totals[i + half])


SENT = (3, 2, 1)


def send_kernel(data_ref, sketch_ref, out3, out2, out1, terms_ref, weights_ref, data, sketch, sems):
    load = pltpu.make_async_copy(sketch_ref, sketch, sems.at[len(SENT) * CHUNKS])
    load.start()

    def prepare():
        load.wait()
        high, low = split(sketch[...])
        both = jnp.concatenate([high.astype(F32), low.astype(F32)], axis=0)
        weights_ref[...] = both.T.astype(BF16)

    sample_quarters(data_ref, SENT, weights_ref, (out3, out2, out1), terms_ref, data, sems, prepare)


def keep_kernel(data_ref, weights_ref, out_ref, terms_ref, data, sems):
    sample_quarters(data_ref, (0,), weights_ref, (out_ref,), terms_ref, data, sems, lambda: None)


def partial_samples(data_slab, sketch_t):
    rows, columns = data_slab.shape
    quarter = rows // QUARTERS
    chunk = quarter // CHUNKS
    sample = jax.ShapeDtypeStruct((chunk, LANES), F32)

    def cost(count):
        return pl.CostEstimate(
            flops=8 * count * quarter * columns * K, bytes_accessed=4 * count * quarter * columns, transcendentals=0
        )

    def scratch(count):
        return [VMEM((count * CHUNKS, chunk, columns), F32)]

    *sent, sent_terms, weights = pl.pallas_call(
        send_kernel,
        out_shape=[sample] * len(SENT)
        + [
            jax.ShapeDtypeStruct((2 * len(SENT) * quarter, columns), BF16),
            jax.ShapeDtypeStruct((columns, LANES), BF16),
        ],
        in_specs=[pl.BlockSpec(memory_space=pltpu.HBM)] * 2,
        out_specs=vmem(len(SENT) + 2),
        scratch_shapes=scratch(len(SENT))
        + [VMEM((K, columns), F32), pltpu.SemaphoreType.DMA((len(SENT) * CHUNKS + 1,))],
        compiler_params=pltpu.CompilerParams(vmem_limit_bytes=42 * MIB),
        cost_estimate=cost(len(SENT)),
    )(in_hbm(data_slab), in_hbm(sketch_t))
    kept, kept_terms = pl.pallas_call(
        keep_kernel,
        out_shape=[sample, jax.ShapeDtypeStruct((2 * quarter, columns), BF16)],
        in_specs=[pl.BlockSpec(memory_space=pltpu.HBM)] + vmem(1),
        out_specs=vmem(2),
        scratch_shapes=scratch(1) + [pltpu.SemaphoreType.DMA((CHUNKS,))],
        compiler_params=pltpu.CompilerParams(vmem_limit_bytes=40 * MIB),
        cost_estimate=cost(1),
    )(in_hbm(data_slab), weights)
    return sent, sent_terms, kept, kept_terms


def left_of(sample):
    high, low = split(unpacked(sample).T)
    left = jnp.concatenate([high, low], axis=0)
    return left, jnp.concatenate([left, left], axis=1)


def term_kernel(sample_ref, terms_ref, *refs):
    out_ref = refs[-1]
    _, left = left_of(sample_ref[...])
    width = out_ref.shape[1] // GROUPS
    for g in range(GROUPS):
        at = pl.ds(g * width, width)
        total = jnp.dot(left, terms_ref[:, at], preferred_element_type=F32)
        total = total[:K] + total[K:]
        for ref in refs[:-1]:
            total += ref[:, at]
        out_ref[:, at] = total


def next_term_kernel(index, sample_ref, terms_ref, begun_ref, out_ref):
    size = terms_ref.shape[0] // len(SENT)
    term_kernel(sample_ref, terms_ref.at[pl.ds(index * size, size)], begun_ref, out_ref)


def half_blocks(first_group, index, sample_ref, terms_ref, begun_ref, out_ref):
    size = terms_ref.shape[0] // len(SENT)
    _, left = left_of(sample_ref[...])
    width = PER_GROUP * LANES
    for g in range(PER_GROUP):
        at = pl.ds(pl.multiple_of(group_place(first_group + g) * width, width), width)
        total = jnp.dot(left, terms_ref[pl.ds(index * size, size), at], preferred_element_type=F32)
        total = total[:K] + total[K:] + begun_ref[:, at]
        for t in range(PER_GROUP):
            out_ref[pl.ds((g * PER_GROUP + t) * K, K), :] = total[:, t * LANES : (t + 1) * LANES]


def sent_half_kernel(index, s0, s3, s2, s1, terms_ref, begun_ref, out_ref):
    every = jnp.concatenate([left_of(ref[...])[0] for ref in (s0, s3, s2, s1)], axis=1)
    gram = lax.dot_general(every, every, (((1,), (1,)), ((), ())), preferred_element_type=F32)
    gram = gram[:K] + gram[K:]
    gram = gram + pltpu.roll(gram, K, axis=1)
    lane = lax.broadcasted_iota(jnp.int32, (K // 2, LANES), 1)
    out_ref[BLOCKS // 2 * K :, :] = jnp.where(lane < K, gram[: K // 2], gram[K // 2 :])
    half_blocks(PER_GROUP, index, (s3, s2, s1)[index], terms_ref, begun_ref, out_ref)


def kept_half_kernel(index, sample_ref, terms_ref, begun_ref, sent_ref, out_ref):
    out_ref[BLOCKS // 2 * K :, :] = sent_ref[BLOCKS // 2 * K :, :]
    half_blocks(0, index, sample_ref, terms_ref, begun_ref, out_ref)


def term_cost(rows, columns):
    return pl.CostEstimate(flops=8 * K * rows * columns, bytes_accessed=4 * rows * columns, transcendentals=0)


def term_call(kernel, shape, operands, cost):
    return pl.pallas_call(
        kernel,
        out_shape=jax.ShapeDtypeStruct(shape, F32),
        in_specs=vmem(len(operands)),
        out_specs=vmem(1)[0],
        compiler_params=pltpu.CompilerParams(vmem_limit_bytes=16 * MIB),
        cost_estimate=cost,
    )(*operands)


def terms_of(quarters, kept_terms, sent_terms):
    size, columns = kept_terms.shape
    cost, less = term_cost(size // 2, columns), term_cost(size // 4, columns)
    whole = (K, columns)
    blocks = (BLOCKS // 2 * K + K // 2, LANES)
    begun = term_call(term_kernel, whole, (quarters[0], kept_terms), cost)
    for index in (0, 2):
        kernel = functools.partial(next_term_kernel, index)
        begun = term_call(kernel, whole, (quarters[1 + index], sent_terms, begun), cost)
    sent = term_call(functools.partial(sent_half_kernel, 1), blocks, (*quarters, sent_terms, begun), less)
    kernel = functools.partial(kept_half_kernel, 1)
    kept = term_call(kernel, blocks, (quarters[2], sent_terms, begun, sent), less)
    return kept, sent


def inverse_kernel(gram_ref, inverse_ref):
    lane = lax.broadcasted_iota(jnp.int32, (K // 2, LANES), 1)
    row = lax.broadcasted_iota(jnp.int32, (K // 2, LANES), 0)
    upper = gram_ref[...]
    lower = pltpu.roll(upper, K, axis=1)
    work = jnp.concatenate(
        [
            jnp.where(lane < K, upper, jnp.where(lane == row + K, 1.0, 0.0)),
            jnp.where(lane < K, lower, jnp.where(lane == row + K + K // 2, 1.0, 0.0)),
        ],
        axis=0,
    )
    count = K // 8
    parts = [work[8 * i : 8 * i + 8] for i in range(count)]
    sub = lax.broadcasted_iota(jnp.int32, (8, LANES), 0)
    diagonal = [jnp.ones((8, LANES), F32)] * count

    def full(value):
        return jnp.broadcast_to(value, (8, LANES))

    for j in range(0, K, 4):
        block, at = divmod(j, 8)
        own = parts[block]
        c1, c2, c3, c4 = [[full(parts[i][:, j + c : j + c + 1]) for i in range(block, count)] for c in range(4)]
        r1, r2, r3, r4 = [full(own[at + r : at + r + 1]) for r in range(4)]
        a11, a12, a13, a14 = [full(c[0][at : at + 1]) for c in (c1, c2, c3, c4)]
        a22, a23, a24 = [full(c[0][at + 1 : at + 2]) for c in (c2, c3, c4)]
        a33, a34 = [full(c[0][at + 2 : at + 3]) for c in (c3, c4)]
        a44 = full(c4[0][at + 3 : at + 4])
        first = a11 * a22 - a12 * a12
        scale = 1.0 / first
        l31, l32 = (a22 * a13 - a12 * a23) * scale, (a11 * a23 - a12 * a13) * scale
        l41, l42 = (a22 * a14 - a12 * a24) * scale, (a11 * a24 - a12 * a14) * scale
        s33 = a33 - (l31 * a13 + l32 * a23)
        s34 = a34 - (l31 * a14 + l32 * a24)
        s44 = a44 - (l41 * a14 + l42 * a24)
        r3 = r3 - (l31 * r1 + l32 * r2)
        r4 = r4 - (l41 * r1 + l42 * r2)
        second = s33 * s44 - s34 * s34
        again = 1.0 / second
        v1, v2 = (a22 * r1 - a12 * r2) * scale, (a11 * r2 - a12 * r1) * scale
        v3, v4 = (s44 * r3 - s34 * r4) * again, (s33 * r4 - s34 * r3) * again
        p1, p3 = 1.0 / a11, 1.0 / s33
        rows = (r2 - a12 * p1 * r1, r3, r4 - s34 * p3 * r3)
        diag = (a11, first * p1, s33, second * p3)
        for r in range(4):
            diagonal[block] = jnp.where(sub == at + r, diag[r], diagonal[block])
        for i in range(block, count):
            f1, f2, f3, f4 = [c[i - block] for c in (c1, c2, c3, c4)]
            f3 = f3 - (f1 * l31 + f2 * l32)
            f4 = f4 - (f1 * l41 + f2 * l42)
            new = parts[i] - ((f1 * v1 + f2 * v2) + (f3 * v3 + f4 * v4))
            if i == block:
                new = jnp.where(sub > at + 3, new, own)
                for r in range(3):
                    new = jnp.where(sub == at + 1 + r, rows[r], new)
            parts[i] = new
    parts = [part * (1.0 / jnp.sqrt(diag)) for part, diag in zip(parts, diagonal)]
    inverse_ref[...] = jnp.concatenate(parts, axis=0)[:, K:]


def inverse_of(gram):
    return pl.pallas_call(
        inverse_kernel,
        out_shape=jax.ShapeDtypeStruct((K, K), F32),
        in_specs=vmem(1),
        out_specs=vmem(1)[0],
        compiler_params=pltpu.CompilerParams(vmem_limit_bytes=8 * MIB),
        cost_estimate=pl.CostEstimate(flops=K**3 * 100, bytes_accessed=8 * K * K, transcendentals=K),
    )(gram)


def basis_kernel(scale, inverse_ref, s0, s3, s2, s1, basis_ref, sample):
    half = s0.shape[0]
    mine = own_quarter()
    for mask, ref in ((0, s0), (3, s3), (2, s2), (1, s1)):
        start = pl.multiple_of((mine ^ mask) * 2 * half, 2 * half)
        sample[pl.ds(start, half), :] = ref[:, :K]
        sample[pl.ds(start + half, half), :] = ref[:, K:]
    basis_ref[...] = lax.dot_general(
        inverse_ref[...] * scale,
        sample[...],
        (((1,), (1,)), ((), ())),
        precision=lax.Precision.HIGHEST,
        preferred_element_type=F32,
    )


def basis_of(inverse, quarters, rows, scale):
    return pl.pallas_call(
        functools.partial(basis_kernel, scale),
        out_shape=jax.ShapeDtypeStruct((K, rows), F32),
        in_specs=vmem(1 + len(quarters)),
        out_specs=vmem(1)[0],
        scratch_shapes=[VMEM((rows, K), F32)],
        compiler_params=pltpu.CompilerParams(vmem_limit_bytes=8 * MIB),
        cost_estimate=pl.CostEstimate(flops=12 * rows * K * K, bytes_accessed=8 * rows * K, transcendentals=0),
    )(inverse, *quarters)


def apply_kernel(first_group, inverse_ref, value_ref, *refs):
    out_ref, parts, sems = refs[-3:]
    high, low = split(inverse_ref[...])
    left = jnp.concatenate([high, low, high], axis=1)
    width = PER_GROUP * LANES
    copies = []
    for g in range(PER_GROUP):
        rows = [value_ref[pl.ds((g * PER_GROUP + t) * K, K), :] for t in range(PER_GROUP)]
        high, low = split(jnp.concatenate(rows, axis=1))
        right = jnp.concatenate([high, high, low], axis=0)
        parts[g] = jnp.dot(left, right, preferred_element_type=F32)
        at = pl.ds(pl.multiple_of(group_place(first_group + g) * width, width), width)
        copies.append(pltpu.make_async_copy(parts.at[g], out_ref.at[:, at], sems.at[g]))
        copies[g].start()
    for copy in copies:
        copy.wait()


def applied(first_group, inverse, value, begun=None):
    columns = BLOCKS * LANES
    more = [] if begun is None else [begun]
    return pl.pallas_call(
        functools.partial(apply_kernel, first_group),
        out_shape=jax.ShapeDtypeStruct((K, columns), F32),
        in_specs=vmem(2) + [pl.BlockSpec(memory_space=pl.ANY)] * len(more),
        out_specs=pl.BlockSpec(memory_space=pl.ANY),
        input_output_aliases={2: 0} if more else {},
        scratch_shapes=[VMEM((PER_GROUP, K, PER_GROUP * LANES), F32), pltpu.SemaphoreType.DMA((PER_GROUP,))],
        compiler_params=pltpu.CompilerParams(vmem_limit_bytes=8 * MIB),
        cost_estimate=pl.CostEstimate(flops=3 * columns * K * K, bytes_accessed=4 * columns * K, transcendentals=0),
    )(inverse, value, *more)


def along_col(value, mask):
    return lax.ppermute(value, "col", [(i, i ^ mask) for i in range(8)])


def along_row(value, masks):
    return lax.ppermute(value, "row", [(i, i ^ masks[i % 2]) for i in range(32)])


CORE = (1, 1)
FIRST = [(t << 3, t << 1) for t in range(4)]
SECOND = [(t << 1, t << 3) for t in range(4)]


def body(data_slab, sketch):
    rows = data_slab.shape[0]
    sent, sent_terms, kept, kept_terms = partial_samples(data_slab, sketch.T)
    got = [along_col(part, mask) for part, mask in zip(sent, SENT)]
    own = kept + got[0] + got[1] + got[2]
    own = own + along_col(own, 7)
    quarters = [own] + [along_col(own, mask) for mask in SENT]

    keep, send = terms_of(quarters, kept_terms, sent_terms)
    total = keep + along_row(send, CORE)
    size = PER_GROUP * K
    gram = total[4 * size :]
    got = [along_row(jnp.concatenate([total[t * size : (t + 1) * size], gram]), FIRST[t]) for t in (1, 2, 3)]
    total = jnp.concatenate([total[:size], gram]) + got[0] + got[1] + got[2]
    got = [along_row(total, SECOND[t]) for t in (1, 2, 3)]
    total = total + got[0] + got[1] + got[2]

    inverse = inverse_of(total[size:])
    block = total[:size]
    mine = jnp.concatenate([block] + [along_row(block, FIRST[t]) for t in (1, 2, 3)])
    range_basis = basis_of(inverse, quarters, rows, math.sqrt(rows * lax.axis_size("row")))
    mine, inverse, range_basis = lax.optimization_barrier((mine, inverse, range_basis))
    theirs = along_row(mine, CORE)
    projected = applied(PER_GROUP, inverse, theirs, applied(0, inverse, mine))
    return range_basis.T, projected


def solution(mesh):
    placed = (P("row", "col"), P("col", None))
    return jax.shard_map(
        body,
        mesh=mesh,
        in_specs=placed,
        out_specs=(P("row", None), P(None, "col")),
        check_vma=False,
    )
```

```python
import functools
import math

import jax
import jax.numpy as jnp
from jax import lax
from jax.experimental import pallas as pl
from jax.experimental.pallas import tpu as pltpu
from jax.sharding import PartitionSpec as P

F32 = jnp.float32
BF16 = jnp.bfloat16
VMEM = pltpu.VMEM
MIB = 2**20
K = 64
LANES = 128
QUARTERS = 4
CHUNKS = 2
BLOCKS = 32
GROUPS = 8
PER_GROUP = 4


def split(value):
    high = value.astype(BF16)
    return high, (value - high.astype(F32)).astype(BF16)


def own_quarter():
    z = lax.axis_index("col")
    return jnp.where(z < QUARTERS, z, 2 * QUARTERS - 1 - z)


def position():
    row = lax.axis_index("row")
    core, y, x = row % 2, (row // 2) % 4, row // 8
    return core, jnp.where(core == 0, x, y), jnp.where(core == 0, y, x)


def group_place(group):
    core, first, second = position()
    if group < PER_GROUP:
        return core * PER_GROUP + (first ^ group)
    return (1 - core) * PER_GROUP + (second ^ (group - PER_GROUP))


def in_hbm(value):
    return pltpu.with_memory_space_constraint(value, pltpu.HBM)


def vmem(count):
    return [pl.BlockSpec(memory_space=VMEM)] * count


def unpacked(value):
    return jnp.concatenate([value[:, :K], value[:, K:]], axis=0)


def sample_quarters(data_ref, masks, weights, outs, terms_ref, data, sems, prepare):
    chunk = data.shape[1]
    rows = CHUNKS * chunk
    mine = own_quarter()
    copies = []
    for i in range(len(masks) * CHUNKS):
        start = pl.multiple_of((mine ^ masks[i // CHUNKS]) * rows + i % CHUNKS * chunk, chunk)
        copies.append(pltpu.make_async_copy(data_ref.at[pl.ds(start, chunk)], data.at[i], sems.at[i]))
        copies[i].start()
    prepare()
    lane = lax.broadcasted_iota(jnp.int32, (chunk, LANES), 1)
    for q in range(len(masks)):
        totals = []
        for i in range(CHUNKS):
            at = q * CHUNKS + i
            copies[at].wait()
            high, low = split(data[at])
            terms_ref[pl.ds(2 * q * rows + i * chunk, chunk), :] = high
            terms_ref[pl.ds((2 * q + 1) * rows + i * chunk, chunk), :] = low
            total = jnp.dot(jnp.concatenate([high, low], axis=0), weights[...], preferred_element_type=F32)
            total = total[:chunk] + total[chunk:]
            totals.append(total + pltpu.roll(total, K, axis=1))
        half = CHUNKS // 2
        for i in range(half):
            outs[q][pl.ds(i * chunk, chunk), :] = jnp.where(lane < K, totals[i], totals[i + half])


SENT = (3, 2, 1)


def send_kernel(data_ref, sketch_ref, out3, out2, out1, terms_ref, weights_ref, data, sketch, sems):
    load = pltpu.make_async_copy(sketch_ref, sketch, sems.at[len(SENT) * CHUNKS])
    load.start()

    def prepare():
        load.wait()
        high, low = split(sketch[...])
        both = jnp.concatenate([high.astype(F32), low.astype(F32)], axis=0)
        weights_ref[...] = both.T.astype(BF16)

    sample_quarters(data_ref, SENT, weights_ref, (out3, out2, out1), terms_ref, data, sems, prepare)


def keep_kernel(data_ref, weights_ref, out_ref, terms_ref, data, sems):
    sample_quarters(data_ref, (0,), weights_ref, (out_ref,), terms_ref, data, sems, lambda: None)


def partial_samples(data_slab, sketch_t):
    rows, columns = data_slab.shape
    quarter = rows // QUARTERS
    chunk = quarter // CHUNKS
    sample = jax.ShapeDtypeStruct((chunk, LANES), F32)

    def cost(count):
        return pl.CostEstimate(
            flops=8 * count * quarter * columns * K, bytes_accessed=4 * count * quarter * columns, transcendentals=0
        )

    def scratch(count):
        return [VMEM((count * CHUNKS, chunk, columns), F32)]

    *sent, sent_terms, weights = pl.pallas_call(
        send_kernel,
        out_shape=[sample] * len(SENT)
        + [
            jax.ShapeDtypeStruct((2 * len(SENT) * quarter, columns), BF16),
            jax.ShapeDtypeStruct((columns, LANES), BF16),
        ],
        in_specs=[pl.BlockSpec(memory_space=pltpu.HBM)] * 2,
        out_specs=vmem(len(SENT) + 2),
        scratch_shapes=scratch(len(SENT))
        + [VMEM((K, columns), F32), pltpu.SemaphoreType.DMA((len(SENT) * CHUNKS + 1,))],
        compiler_params=pltpu.CompilerParams(vmem_limit_bytes=42 * MIB),
        cost_estimate=cost(len(SENT)),
    )(in_hbm(data_slab), in_hbm(sketch_t))
    kept, kept_terms = pl.pallas_call(
        keep_kernel,
        out_shape=[sample, jax.ShapeDtypeStruct((2 * quarter, columns), BF16)],
        in_specs=[pl.BlockSpec(memory_space=pltpu.HBM)] + vmem(1),
        out_specs=vmem(2),
        scratch_shapes=scratch(1) + [pltpu.SemaphoreType.DMA((CHUNKS,))],
        compiler_params=pltpu.CompilerParams(vmem_limit_bytes=40 * MIB),
        cost_estimate=cost(1),
    )(in_hbm(data_slab), weights)
    return sent, sent_terms, kept, kept_terms


def left_of(sample):
    high, low = split(unpacked(sample).T)
    left = jnp.concatenate([high, low], axis=0)
    return left, jnp.concatenate([left, left], axis=1)


def term_kernel(sample_ref, terms_ref, *refs):
    out_ref = refs[-1]
    _, left = left_of(sample_ref[...])
    width = out_ref.shape[1] // GROUPS
    for g in range(GROUPS):
        at = pl.ds(g * width, width)
        total = jnp.dot(left, terms_ref[:, at], preferred_element_type=F32)
        total = total[:K] + total[K:]
        for ref in refs[:-1]:
            total += ref[:, at]
        out_ref[:, at] = total


def next_term_kernel(index, sample_ref, terms_ref, begun_ref, out_ref):
    size = terms_ref.shape[0] // len(SENT)
    term_kernel(sample_ref, terms_ref.at[pl.ds(index * size, size)], begun_ref, out_ref)


def half_blocks(first_group, index, sample_ref, terms_ref, begun_ref, out_ref):
    size = terms_ref.shape[0] // len(SENT)
    _, left = left_of(sample_ref[...])
    width = PER_GROUP * LANES
    for g in range(PER_GROUP):
        at = pl.ds(pl.multiple_of(group_place(first_group + g) * width, width), width)
        total = jnp.dot(left, terms_ref[pl.ds(index * size, size), at], preferred_element_type=F32)
        total = total[:K] + total[K:] + begun_ref[:, at]
        for t in range(PER_GROUP):
            out_ref[pl.ds((g * PER_GROUP + t) * K, K), :] = total[:, t * LANES : (t + 1) * LANES]


def sent_half_kernel(index, s0, s3, s2, s1, terms_ref, begun_ref, out_ref):
    every = jnp.concatenate([left_of(ref[...])[0] for ref in (s0, s3, s2, s1)], axis=1)
    gram = lax.dot_general(every, every, (((1,), (1,)), ((), ())), preferred_element_type=F32)
    gram = gram[:K] + gram[K:]
    gram = gram + pltpu.roll(gram, K, axis=1)
    lane = lax.broadcasted_iota(jnp.int32, (K // 2, LANES), 1)
    out_ref[BLOCKS // 2 * K :, :] = jnp.where(lane < K, gram[: K // 2], gram[K // 2 :])
    half_blocks(PER_GROUP, index, (s3, s2, s1)[index], terms_ref, begun_ref, out_ref)


def kept_half_kernel(index, sample_ref, terms_ref, begun_ref, sent_ref, out_ref):
    out_ref[BLOCKS // 2 * K :, :] = sent_ref[BLOCKS // 2 * K :, :]
    half_blocks(0, index, sample_ref, terms_ref, begun_ref, out_ref)


def term_cost(rows, columns):
    return pl.CostEstimate(flops=8 * K * rows * columns, bytes_accessed=4 * rows * columns, transcendentals=0)


def term_call(kernel, shape, operands, cost):
    return pl.pallas_call(
        kernel,
        out_shape=jax.ShapeDtypeStruct(shape, F32),
        in_specs=vmem(len(operands)),
        out_specs=vmem(1)[0],
        compiler_params=pltpu.CompilerParams(vmem_limit_bytes=16 * MIB),
        cost_estimate=cost,
    )(*operands)


def terms_of(quarters, kept_terms, sent_terms):
    size, columns = kept_terms.shape
    cost, less = term_cost(size // 2, columns), term_cost(size // 4, columns)
    whole = (K, columns)
    blocks = (BLOCKS // 2 * K + K // 2, LANES)
    begun = term_call(term_kernel, whole, (quarters[0], kept_terms), cost)
    for index in (0, 2):
        kernel = functools.partial(next_term_kernel, index)
        begun = term_call(kernel, whole, (quarters[1 + index], sent_terms, begun), cost)
    sent = term_call(functools.partial(sent_half_kernel, 1), blocks, (*quarters, sent_terms, begun), less)
    kernel = functools.partial(kept_half_kernel, 1)
    kept = term_call(kernel, blocks, (quarters[2], sent_terms, begun, sent), less)
    return kept, sent


def inverse_kernel(gram_ref, inverse_ref):
    lane = lax.broadcasted_iota(jnp.int32, (K // 2, LANES), 1)
    row = lax.broadcasted_iota(jnp.int32, (K // 2, LANES), 0)
    upper = gram_ref[...]
    lower = pltpu.roll(upper, K, axis=1)
    work = jnp.concatenate(
        [
            jnp.where(lane < K, upper, jnp.where(lane == row + K, 1.0, 0.0)),
            jnp.where(lane < K, lower, jnp.where(lane == row + K + K // 2, 1.0, 0.0)),
        ],
        axis=0,
    )
    count = K // 8
    parts = [work[8 * i : 8 * i + 8] for i in range(count)]
    sub = lax.broadcasted_iota(jnp.int32, (8, LANES), 0)
    diagonal = [jnp.ones((8, LANES), F32)] * count

    def full(value):
        return jnp.broadcast_to(value, (8, LANES))

    for j in range(0, K, 4):
        block, at = divmod(j, 8)
        own = parts[block]
        c1, c2, c3, c4 = [[full(parts[i][:, j + c : j + c + 1]) for i in range(block, count)] for c in range(4)]
        r1, r2, r3, r4 = [full(own[at + r : at + r + 1]) for r in range(4)]
        a11, a12, a13, a14 = [full(c[0][at : at + 1]) for c in (c1, c2, c3, c4)]
        a22, a23, a24 = [full(c[0][at + 1 : at + 2]) for c in (c2, c3, c4)]
        a33, a34 = [full(c[0][at + 2 : at + 3]) for c in (c3, c4)]
        a44 = full(c4[0][at + 3 : at + 4])
        first = a11 * a22 - a12 * a12
        scale = 1.0 / first
        l31, l32 = (a22 * a13 - a12 * a23) * scale, (a11 * a23 - a12 * a13) * scale
        l41, l42 = (a22 * a14 - a12 * a24) * scale, (a11 * a24 - a12 * a14) * scale
        s33 = a33 - (l31 * a13 + l32 * a23)
        s34 = a34 - (l31 * a14 + l32 * a24)
        s44 = a44 - (l41 * a14 + l42 * a24)
        r3 = r3 - (l31 * r1 + l32 * r2)
        r4 = r4 - (l41 * r1 + l42 * r2)
        second = s33 * s44 - s34 * s34
        again = 1.0 / second
        v1, v2 = (a22 * r1 - a12 * r2) * scale, (a11 * r2 - a12 * r1) * scale
        v3, v4 = (s44 * r3 - s34 * r4) * again, (s33 * r4 - s34 * r3) * again
        p1, p3 = 1.0 / a11, 1.0 / s33
        rows = (r2 - a12 * p1 * r1, r3, r4 - s34 * p3 * r3)
        diag = (a11, first * p1, s33, second * p3)
        for r in range(4):
            diagonal[block] = jnp.where(sub == at + r, diag[r], diagonal[block])
        for i in range(block, count):
            f1, f2, f3, f4 = [c[i - block] for c in (c1, c2, c3, c4)]
            f3 = f3 - (f1 * l31 + f2 * l32)
            f4 = f4 - (f1 * l41 + f2 * l42)
            new = parts[i] - ((f1 * v1 + f2 * v2) + (f3 * v3 + f4 * v4))
            if i == block:
                new = jnp.where(sub > at + 3, new, own)
                for r in range(3):
                    new = jnp.where(sub == at + 1 + r, rows[r], new)
            parts[i] = new
    parts = [part * (1.0 / jnp.sqrt(diag)) for part, diag in zip(parts, diagonal)]
    inverse_ref[...] = jnp.concatenate(parts, axis=0)[:, K:]


def inverse_of(gram):
    return pl.pallas_call(
        inverse_kernel,
        out_shape=jax.ShapeDtypeStruct((K, K), F32),
        in_specs=vmem(1),
        out_specs=vmem(1)[0],
        compiler_params=pltpu.CompilerParams(vmem_limit_bytes=8 * MIB),
        cost_estimate=pl.CostEstimate(flops=K**3 * 100, bytes_accessed=8 * K * K, transcendentals=K),
    )(gram)


def basis_kernel(scale, inverse_ref, s0, s3, s2, s1, basis_ref, sample):
    half = s0.shape[0]
    mine = own_quarter()
    for mask, ref in ((0, s0), (3, s3), (2, s2), (1, s1)):
        start = pl.multiple_of((mine ^ mask) * 2 * half, 2 * half)
        sample[pl.ds(start, half), :] = ref[:, :K]
        sample[pl.ds(start + half, half), :] = ref[:, K:]
    basis_ref[...] = lax.dot_general(
        inverse_ref[...] * scale,
        sample[...],
        (((1,), (1,)), ((), ())),
        precision=lax.Precision.HIGHEST,
        preferred_element_type=F32,
    )


def basis_of(inverse, quarters, rows, scale):
    return pl.pallas_call(
        functools.partial(basis_kernel, scale),
        out_shape=jax.ShapeDtypeStruct((K, rows), F32),
        in_specs=vmem(1 + len(quarters)),
        out_specs=vmem(1)[0],
        scratch_shapes=[VMEM((rows, K), F32)],
        compiler_params=pltpu.CompilerParams(vmem_limit_bytes=8 * MIB),
        cost_estimate=pl.CostEstimate(flops=12 * rows * K * K, bytes_accessed=8 * rows * K, transcendentals=0),
    )(inverse, *quarters)


def apply_kernel(first_group, inverse_ref, value_ref, *refs):
    out_ref, parts, sems = refs[-3:]
    high, low = split(inverse_ref[...])
    left = jnp.concatenate([high, low, high], axis=1)
    width = PER_GROUP * LANES
    copies = []
    for g in range(PER_GROUP):
        rows = [value_ref[pl.ds((g * PER_GROUP + t) * K, K), :] for t in range(PER_GROUP)]
        high, low = split(jnp.concatenate(rows, axis=1))
        right = jnp.concatenate([high, high, low], axis=0)
        parts[g] = jnp.dot(left, right, preferred_element_type=F32)
        at = pl.ds(pl.multiple_of(group_place(first_group + g) * width, width), width)
        copies.append(pltpu.make_async_copy(parts.at[g], out_ref.at[:, at], sems.at[g]))
        copies[g].start()
    for copy in copies:
        copy.wait()


def applied(first_group, inverse, value, begun=None):
    columns = BLOCKS * LANES
    more = [] if begun is None else [begun]
    return pl.pallas_call(
        functools.partial(apply_kernel, first_group),
        out_shape=jax.ShapeDtypeStruct((K, columns), F32),
        in_specs=vmem(2) + [pl.BlockSpec(memory_space=pl.ANY)] * len(more),
        out_specs=pl.BlockSpec(memory_space=pl.ANY),
        input_output_aliases={2: 0} if more else {},
        scratch_shapes=[VMEM((PER_GROUP, K, PER_GROUP * LANES), F32), pltpu.SemaphoreType.DMA((PER_GROUP,))],
        compiler_params=pltpu.CompilerParams(vmem_limit_bytes=8 * MIB),
        cost_estimate=pl.CostEstimate(flops=3 * columns * K * K, bytes_accessed=4 * columns * K, transcendentals=0),
    )(inverse, value, *more)


def along_col(value, mask):
    return lax.ppermute(value, "col", [(i, i ^ mask) for i in range(8)])


def along_row(value, masks):
    return lax.ppermute(value, "row", [(i, i ^ masks[i % 2]) for i in range(32)])


CORE = (1, 1)
FIRST = [(t << 3, t << 1) for t in range(4)]
SECOND = [(t << 1, t << 3) for t in range(4)]


def body(data_slab, sketch):
    rows = data_slab.shape[0]
    sent, sent_terms, kept, kept_terms = partial_samples(data_slab, sketch.T)
    got = [along_col(part, mask) for part, mask in zip(sent, SENT)]
    own = kept + got[0] + got[1] + got[2]
    own = own + along_col(own, 7)
    quarters = [own] + [along_col(own, mask) for mask in SENT]

    keep, send = terms_of(quarters, kept_terms, sent_terms)
    total = keep + along_row(send, CORE)
    size = PER_GROUP * K
    gram = total[4 * size :]
    got = [along_row(jnp.concatenate([total[t * size : (t + 1) * size], gram]), FIRST[t]) for t in (2, 1, 3)]
    total = jnp.concatenate([total[:size], gram]) + got[0] + got[1] + got[2]
    got = [along_row(total, SECOND[t]) for t in (1, 2, 3)]
    total = total + got[0] + got[1] + got[2]

    inverse = inverse_of(total[size:])
    block = total[:size]
    mine = jnp.concatenate([block] + [along_row(block, FIRST[t]) for t in (1, 2, 3)])
    range_basis = basis_of(inverse, quarters, rows, math.sqrt(rows * lax.axis_size("row")))
    mine, inverse, range_basis = lax.optimization_barrier((mine, inverse, range_basis))
    theirs = along_row(mine, CORE)
    projected = applied(PER_GROUP, inverse, theirs, applied(0, inverse, mine))
    return range_basis.T, projected


def solution(mesh):
    placed = (P("row", "col"), P("col", None))
    return jax.shard_map(
        body,
        mesh=mesh,
        in_specs=placed,
        out_specs=(P("row", None), P(None, "col")),
        check_vma=False,
    )
```

```python
import functools
import math

import jax
import jax.numpy as jnp
from jax import lax
from jax.experimental import pallas as pl
from jax.experimental.pallas import tpu as pltpu
from jax.sharding import PartitionSpec as P

F32 = jnp.float32
BF16 = jnp.bfloat16
VMEM = pltpu.VMEM
MIB = 2**20
K = 64
LANES = 128
QUARTERS = 4
CHUNKS = 2
BLOCKS = 32
GROUPS = 8
PER_GROUP = 4


def split(value):
    high = value.astype(BF16)
    return high, (value - high.astype(F32)).astype(BF16)


def own_quarter():
    z = lax.axis_index("col")
    return jnp.where(z < QUARTERS, z, 2 * QUARTERS - 1 - z)


def position():
    row = lax.axis_index("row")
    core, y, x = row % 2, (row // 2) % 4, row // 8
    return core, jnp.where(core == 0, x, y), jnp.where(core == 0, y, x)


def group_place(group):
    core, first, second = position()
    if group < PER_GROUP:
        return core * PER_GROUP + (first ^ group)
    return (1 - core) * PER_GROUP + (second ^ (group - PER_GROUP))


def in_hbm(value):
    return pltpu.with_memory_space_constraint(value, pltpu.HBM)


def vmem(count):
    return [pl.BlockSpec(memory_space=VMEM)] * count


def unpacked(value):
    return jnp.concatenate([value[:, :K], value[:, K:]], axis=0)


def sample_quarters(data_ref, masks, weights, outs, terms_ref, data, sems, prepare):
    chunk = data.shape[1]
    rows = CHUNKS * chunk
    mine = own_quarter()
    copies = []
    for i in range(len(masks) * CHUNKS):
        start = pl.multiple_of((mine ^ masks[i // CHUNKS]) * rows + i % CHUNKS * chunk, chunk)
        copies.append(pltpu.make_async_copy(data_ref.at[pl.ds(start, chunk)], data.at[i], sems.at[i]))
        copies[i].start()
    prepare()
    lane = lax.broadcasted_iota(jnp.int32, (chunk, LANES), 1)
    for q in range(len(masks)):
        totals = []
        for i in range(CHUNKS):
            at = q * CHUNKS + i
            copies[at].wait()
            high, low = split(data[at])
            terms_ref[pl.ds(2 * q * rows + i * chunk, chunk), :] = high
            terms_ref[pl.ds((2 * q + 1) * rows + i * chunk, chunk), :] = low
            total = jnp.dot(jnp.concatenate([high, low], axis=0), weights[...], preferred_element_type=F32)
            total = total[:chunk] + total[chunk:]
            totals.append(total + pltpu.roll(total, K, axis=1))
        half = CHUNKS // 2
        for i in range(half):
            outs[q][pl.ds(i * chunk, chunk), :] = jnp.where(lane < K, totals[i], totals[i + half])


SENT = (3, 2, 1)


def send_kernel(data_ref, sketch_ref, out3, out2, out1, terms_ref, weights_ref, data, sketch, sems):
    load = pltpu.make_async_copy(sketch_ref, sketch, sems.at[len(SENT) * CHUNKS])
    load.start()

    def prepare():
        load.wait()
        high, low = split(sketch[...])
        both = jnp.concatenate([high.astype(F32), low.astype(F32)], axis=0)
        weights_ref[...] = both.T.astype(BF16)

    sample_quarters(data_ref, SENT, weights_ref, (out3, out2, out1), terms_ref, data, sems, prepare)


def keep_kernel(data_ref, weights_ref, out_ref, terms_ref, data, sems):
    sample_quarters(data_ref, (0,), weights_ref, (out_ref,), terms_ref, data, sems, lambda: None)


def partial_samples(data_slab, sketch_t):
    rows, columns = data_slab.shape
    quarter = rows // QUARTERS
    chunk = quarter // CHUNKS
    sample = jax.ShapeDtypeStruct((chunk, LANES), F32)

    def cost(count):
        return pl.CostEstimate(
            flops=8 * count * quarter * columns * K, bytes_accessed=4 * count * quarter * columns, transcendentals=0
        )

    def scratch(count):
        return [VMEM((count * CHUNKS, chunk, columns), F32)]

    *sent, sent_terms, weights = pl.pallas_call(
        send_kernel,
        out_shape=[sample] * len(SENT)
        + [
            jax.ShapeDtypeStruct((2 * len(SENT) * quarter, columns), BF16),
            jax.ShapeDtypeStruct((columns, LANES), BF16),
        ],
        in_specs=[pl.BlockSpec(memory_space=pltpu.HBM)] * 2,
        out_specs=vmem(len(SENT) + 2),
        scratch_shapes=scratch(len(SENT))
        + [VMEM((K, columns), F32), pltpu.SemaphoreType.DMA((len(SENT) * CHUNKS + 1,))],
        compiler_params=pltpu.CompilerParams(vmem_limit_bytes=42 * MIB),
        cost_estimate=cost(len(SENT)),
    )(in_hbm(data_slab), in_hbm(sketch_t))
    kept, kept_terms = pl.pallas_call(
        keep_kernel,
        out_shape=[sample, jax.ShapeDtypeStruct((2 * quarter, columns), BF16)],
        in_specs=[pl.BlockSpec(memory_space=pltpu.HBM)] + vmem(1),
        out_specs=vmem(2),
        scratch_shapes=scratch(1) + [pltpu.SemaphoreType.DMA((CHUNKS,))],
        compiler_params=pltpu.CompilerParams(vmem_limit_bytes=40 * MIB),
        cost_estimate=cost(1),
    )(in_hbm(data_slab), weights)
    return sent, sent_terms, kept, kept_terms


def left_of(sample):
    high, low = split(unpacked(sample).T)
    left = jnp.concatenate([high, low], axis=0)
    return left, jnp.concatenate([left, left], axis=1)


def term_kernel(sample_ref, terms_ref, *refs):
    out_ref = refs[-1]
    _, left = left_of(sample_ref[...])
    width = out_ref.shape[1] // GROUPS
    for g in range(GROUPS):
        at = pl.ds(g * width, width)
        total = jnp.dot(left, terms_ref[:, at], preferred_element_type=F32)
        total = total[:K] + total[K:]
        for ref in refs[:-1]:
            total += ref[:, at]
        out_ref[:, at] = total


def next_term_kernel(index, sample_ref, terms_ref, begun_ref, out_ref):
    size = terms_ref.shape[0] // len(SENT)
    term_kernel(sample_ref, terms_ref.at[pl.ds(index * size, size)], begun_ref, out_ref)


def half_blocks(first_group, index, sample_ref, terms_ref, begun_ref, out_ref):
    size = terms_ref.shape[0] // len(SENT)
    _, left = left_of(sample_ref[...])
    width = PER_GROUP * LANES
    for g in range(PER_GROUP):
        at = pl.ds(pl.multiple_of(group_place(first_group + g) * width, width), width)
        total = jnp.dot(left, terms_ref[pl.ds(index * size, size), at], preferred_element_type=F32)
        total = total[:K] + total[K:] + begun_ref[:, at]
        for t in range(PER_GROUP):
            out_ref[pl.ds((g * PER_GROUP + t) * K, K), :] = total[:, t * LANES : (t + 1) * LANES]


def sent_half_kernel(index, s0, s3, s2, s1, terms_ref, begun_ref, out_ref):
    every = jnp.concatenate([left_of(ref[...])[0] for ref in (s0, s3, s2, s1)], axis=1)
    gram = lax.dot_general(every, every, (((1,), (1,)), ((), ())), preferred_element_type=F32)
    gram = gram[:K] + gram[K:]
    gram = gram + pltpu.roll(gram, K, axis=1)
    lane = lax.broadcasted_iota(jnp.int32, (K // 2, LANES), 1)
    out_ref[BLOCKS // 2 * K :, :] = jnp.where(lane < K, gram[: K // 2], gram[K // 2 :])
    half_blocks(PER_GROUP, index, (s3, s2, s1)[index], terms_ref, begun_ref, out_ref)


def kept_half_kernel(index, sample_ref, terms_ref, begun_ref, sent_ref, out_ref):
    out_ref[BLOCKS // 2 * K :, :] = sent_ref[BLOCKS // 2 * K :, :]
    half_blocks(0, index, sample_ref, terms_ref, begun_ref, out_ref)


def term_cost(rows, columns):
    return pl.CostEstimate(flops=8 * K * rows * columns, bytes_accessed=4 * rows * columns, transcendentals=0)


def term_call(kernel, shape, operands, cost):
    return pl.pallas_call(
        kernel,
        out_shape=jax.ShapeDtypeStruct(shape, F32),
        in_specs=vmem(len(operands)),
        out_specs=vmem(1)[0],
        compiler_params=pltpu.CompilerParams(vmem_limit_bytes=16 * MIB),
        cost_estimate=cost,
    )(*operands)


def terms_of(quarters, kept_terms, sent_terms):
    size, columns = kept_terms.shape
    cost, less = term_cost(size // 2, columns), term_cost(size // 4, columns)
    whole = (K, columns)
    blocks = (BLOCKS // 2 * K + K // 2, LANES)
    begun = term_call(term_kernel, whole, (quarters[0], kept_terms), cost)
    for index in (0, 1):
        kernel = functools.partial(next_term_kernel, index)
        begun = term_call(kernel, whole, (quarters[1 + index], sent_terms, begun), cost)
    sent = term_call(functools.partial(sent_half_kernel, 2), blocks, (*quarters, sent_terms, begun), less)
    kernel = functools.partial(kept_half_kernel, 2)
    kept = term_call(kernel, blocks, (quarters[3], sent_terms, begun, sent), less)
    return kept, sent


def inverse_kernel(gram_ref, inverse_ref):
    lane = lax.broadcasted_iota(jnp.int32, (K // 2, LANES), 1)
    row = lax.broadcasted_iota(jnp.int32, (K // 2, LANES), 0)
    upper = gram_ref[...]
    lower = pltpu.roll(upper, K, axis=1)
    work = jnp.concatenate(
        [
            jnp.where(lane < K, upper, jnp.where(lane == row + K, 1.0, 0.0)),
            jnp.where(lane < K, lower, jnp.where(lane == row + K + K // 2, 1.0, 0.0)),
        ],
        axis=0,
    )
    count = K // 8
    parts = [work[8 * i : 8 * i + 8] for i in range(count)]
    sub = lax.broadcasted_iota(jnp.int32, (8, LANES), 0)
    diagonal = [jnp.ones((8, LANES), F32)] * count

    def full(value):
        return jnp.broadcast_to(value, (8, LANES))

    for j in range(0, K, 4):
        block, at = divmod(j, 8)
        own = parts[block]
        c1, c2, c3, c4 = [[full(parts[i][:, j + c : j + c + 1]) for i in range(block, count)] for c in range(4)]
        r1, r2, r3, r4 = [full(own[at + r : at + r + 1]) for r in range(4)]
        a11, a12, a13, a14 = [full(c[0][at : at + 1]) for c in (c1, c2, c3, c4)]
        a22, a23, a24 = [full(c[0][at + 1 : at + 2]) for c in (c2, c3, c4)]
        a33, a34 = [full(c[0][at + 2 : at + 3]) for c in (c3, c4)]
        a44 = full(c4[0][at + 3 : at + 4])
        first = a11 * a22 - a12 * a12
        scale = 1.0 / first
        l31, l32 = (a22 * a13 - a12 * a23) * scale, (a11 * a23 - a12 * a13) * scale
        l41, l42 = (a22 * a14 - a12 * a24) * scale, (a11 * a24 - a12 * a14) * scale
        s33 = a33 - (l31 * a13 + l32 * a23)
        s34 = a34 - (l31 * a14 + l32 * a24)
        s44 = a44 - (l41 * a14 + l42 * a24)
        r3 = r3 - (l31 * r1 + l32 * r2)
        r4 = r4 - (l41 * r1 + l42 * r2)
        second = s33 * s44 - s34 * s34
        again = 1.0 / second
        v1, v2 = (a22 * r1 - a12 * r2) * scale, (a11 * r2 - a12 * r1) * scale
        v3, v4 = (s44 * r3 - s34 * r4) * again, (s33 * r4 - s34 * r3) * again
        p1, p3 = 1.0 / a11, 1.0 / s33
        rows = (r2 - a12 * p1 * r1, r3, r4 - s34 * p3 * r3)
        diag = (a11, first * p1, s33, second * p3)
        for r in range(4):
            diagonal[block] = jnp.where(sub == at + r, diag[r], diagonal[block])
        for i in range(block, count):
            f1, f2, f3, f4 = [c[i - block] for c in (c1, c2, c3, c4)]
            f3 = f3 - (f1 * l31 + f2 * l32)
            f4 = f4 - (f1 * l41 + f2 * l42)
            new = parts[i] - ((f1 * v1 + f2 * v2) + (f3 * v3 + f4 * v4))
            if i == block:
                new = jnp.where(sub > at + 3, new, own)
                for r in range(3):
                    new = jnp.where(sub == at + 1 + r, rows[r], new)
            parts[i] = new
    parts = [part * (1.0 / jnp.sqrt(diag)) for part, diag in zip(parts, diagonal)]
    inverse_ref[...] = jnp.concatenate(parts, axis=0)[:, K:]


def inverse_of(gram):
    return pl.pallas_call(
        inverse_kernel,
        out_shape=jax.ShapeDtypeStruct((K, K), F32),
        in_specs=vmem(1),
        out_specs=vmem(1)[0],
        compiler_params=pltpu.CompilerParams(vmem_limit_bytes=8 * MIB),
        cost_estimate=pl.CostEstimate(flops=K**3 * 100, bytes_accessed=8 * K * K, transcendentals=K),
    )(gram)


def basis_kernel(scale, inverse_ref, s0, s3, s2, s1, basis_ref, sample):
    half = s0.shape[0]
    mine = own_quarter()
    for mask, ref in ((0, s0), (3, s3), (2, s2), (1, s1)):
        start = pl.multiple_of((mine ^ mask) * 2 * half, 2 * half)
        sample[pl.ds(start, half), :] = ref[:, :K]
        sample[pl.ds(start + half, half), :] = ref[:, K:]
    basis_ref[...] = lax.dot_general(
        inverse_ref[...] * scale,
        sample[...],
        (((1,), (1,)), ((), ())),
        precision=lax.Precision.HIGHEST,
        preferred_element_type=F32,
    )


def basis_of(inverse, quarters, rows, scale):
    return pl.pallas_call(
        functools.partial(basis_kernel, scale),
        out_shape=jax.ShapeDtypeStruct((K, rows), F32),
        in_specs=vmem(1 + len(quarters)),
        out_specs=vmem(1)[0],
        scratch_shapes=[VMEM((rows, K), F32)],
        compiler_params=pltpu.CompilerParams(vmem_limit_bytes=8 * MIB),
        cost_estimate=pl.CostEstimate(flops=12 * rows * K * K, bytes_accessed=8 * rows * K, transcendentals=0),
    )(inverse, *quarters)


def apply_kernel(first_group, inverse_ref, value_ref, *refs):
    out_ref, parts, sems = refs[-3:]
    high, low = split(inverse_ref[...])
    left = jnp.concatenate([high, low, high], axis=1)
    width = PER_GROUP * LANES
    copies = []
    for g in range(PER_GROUP):
        rows = [value_ref[pl.ds((g * PER_GROUP + t) * K, K), :] for t in range(PER_GROUP)]
        high, low = split(jnp.concatenate(rows, axis=1))
        right = jnp.concatenate([high, high, low], axis=0)
        parts[g] = jnp.dot(left, right, preferred_element_type=F32)
        at = pl.ds(pl.multiple_of(group_place(first_group + g) * width, width), width)
        copies.append(pltpu.make_async_copy(parts.at[g], out_ref.at[:, at], sems.at[g]))
        copies[g].start()
    for copy in copies:
        copy.wait()


def applied(first_group, inverse, value, begun=None):
    columns = BLOCKS * LANES
    more = [] if begun is None else [begun]
    return pl.pallas_call(
        functools.partial(apply_kernel, first_group),
        out_shape=jax.ShapeDtypeStruct((K, columns), F32),
        in_specs=vmem(2) + [pl.BlockSpec(memory_space=pl.ANY)] * len(more),
        out_specs=pl.BlockSpec(memory_space=pl.ANY),
        input_output_aliases={2: 0} if more else {},
        scratch_shapes=[VMEM((PER_GROUP, K, PER_GROUP * LANES), F32), pltpu.SemaphoreType.DMA((PER_GROUP,))],
        compiler_params=pltpu.CompilerParams(vmem_limit_bytes=8 * MIB),
        cost_estimate=pl.CostEstimate(flops=3 * columns * K * K, bytes_accessed=4 * columns * K, transcendentals=0),
    )(inverse, value, *more)


def along_col(value, mask):
    return lax.ppermute(value, "col", [(i, i ^ mask) for i in range(8)])


def along_row(value, masks):
    return lax.ppermute(value, "row", [(i, i ^ masks[i % 2]) for i in range(32)])


CORE = (1, 1)
FIRST = [(t << 3, t << 1) for t in range(4)]
SECOND = [(t << 1, t << 3) for t in range(4)]


def body(data_slab, sketch):
    rows = data_slab.shape[0]
    sent, sent_terms, kept, kept_terms = partial_samples(data_slab, sketch.T)
    got = [along_col(part, mask) for part, mask in zip(sent, SENT)]
    own = kept + got[0] + got[1] + got[2]
    own = own + along_col(own, 7)
    quarters = [own] + [along_col(own, mask) for mask in SENT]

    keep, send = terms_of(quarters, kept_terms, sent_terms)
    total = keep + along_row(send, CORE)
    size = PER_GROUP * K
    gram = total[4 * size :]
    got = [along_row(jnp.concatenate([total[t * size : (t + 1) * size], gram]), FIRST[t]) for t in (2, 1, 3)]
    total = jnp.concatenate([total[:size], gram]) + got[0] + got[1] + got[2]
    got = [along_row(total, SECOND[t]) for t in (1, 2, 3)]
    total = total + got[0] + got[1] + got[2]

    inverse = inverse_of(total[size:])
    block = total[:size]
    mine = jnp.concatenate([block] + [along_row(block, FIRST[t]) for t in (1, 2, 3)])
    range_basis = basis_of(inverse, quarters, rows, math.sqrt(rows * lax.axis_size("row")))
    mine, inverse, range_basis = lax.optimization_barrier((mine, inverse, range_basis))
    theirs = along_row(mine, CORE)
    projected = applied(PER_GROUP, inverse, theirs, applied(0, inverse, mine))
    return range_basis.T, projected


def solution(mesh):
    placed = (P("row", "col"), P("col", None))
    return jax.shard_map(
        body,
        mesh=mesh,
        in_specs=placed,
        out_specs=(P("row", None), P(None, "col")),
        check_vma=False,
    )
```

```python
import functools
import math

import jax
import jax.numpy as jnp
from jax import lax
from jax.experimental import pallas as pl
from jax.experimental.pallas import tpu as pltpu
from jax.sharding import PartitionSpec as P

F32 = jnp.float32
BF16 = jnp.bfloat16
VMEM = pltpu.VMEM
MIB = 2**20
K = 64
LANES = 128
QUARTERS = 4
CHUNKS = 2
BLOCKS = 32
GROUPS = 8
PER_GROUP = 4


def split(value):
    high = value.astype(BF16)
    return high, (value - high.astype(F32)).astype(BF16)


def own_quarter():
    z = lax.axis_index("col")
    return jnp.where(z < QUARTERS, z, 2 * QUARTERS - 1 - z)


def position():
    row = lax.axis_index("row")
    core, y, x = row % 2, (row // 2) % 4, row // 8
    return core, jnp.where(core == 0, x, y), jnp.where(core == 0, y, x)


def group_place(group):
    core, first, second = position()
    if group < PER_GROUP:
        return core * PER_GROUP + (first ^ group)
    return (1 - core) * PER_GROUP + (second ^ (group - PER_GROUP))


def in_hbm(value):
    return pltpu.with_memory_space_constraint(value, pltpu.HBM)


def vmem(count):
    return [pl.BlockSpec(memory_space=VMEM)] * count


def unpacked(value):
    return jnp.concatenate([value[:, :K], value[:, K:]], axis=0)


def sample_quarters(data_ref, masks, weights, outs, terms_ref, data, sems, prepare):
    chunk = data.shape[1]
    rows = CHUNKS * chunk
    mine = own_quarter()
    copies = []
    for i in range(len(masks) * CHUNKS):
        start = pl.multiple_of((mine ^ masks[i // CHUNKS]) * rows + i % CHUNKS * chunk, chunk)
        copies.append(pltpu.make_async_copy(data_ref.at[pl.ds(start, chunk)], data.at[i], sems.at[i]))
        copies[i].start()
    prepare()
    lane = lax.broadcasted_iota(jnp.int32, (chunk, LANES), 1)
    for q in range(len(masks)):
        totals = []
        for i in range(CHUNKS):
            at = q * CHUNKS + i
            copies[at].wait()
            high, low = split(data[at])
            terms_ref[pl.ds(2 * q * rows + i * chunk, chunk), :] = high
            terms_ref[pl.ds((2 * q + 1) * rows + i * chunk, chunk), :] = low
            total = jnp.dot(jnp.concatenate([high, low], axis=0), weights[...], preferred_element_type=F32)
            total = total[:chunk] + total[chunk:]
            totals.append(total + pltpu.roll(total, K, axis=1))
        half = CHUNKS // 2
        for i in range(half):
            outs[q][pl.ds(i * chunk, chunk), :] = jnp.where(lane < K, totals[i], totals[i + half])


SENT = (3, 2, 1)
ORDER = (0, 1, 3, 2)


def send_kernel(data_ref, sketch_ref, out3, out2, out1, terms_ref, weights_ref, data, sketch, sems):
    load = pltpu.make_async_copy(sketch_ref, sketch, sems.at[len(SENT) * CHUNKS])
    load.start()

    def prepare():
        load.wait()
        high, low = split(sketch[...])
        both = jnp.concatenate([high.astype(F32), low.astype(F32)], axis=0)
        weights_ref[...] = both.T.astype(BF16)

    sample_quarters(data_ref, SENT, weights_ref, (out3, out2, out1), terms_ref, data, sems, prepare)


def keep_kernel(data_ref, weights_ref, out_ref, terms_ref, data, sems):
    sample_quarters(data_ref, (0,), weights_ref, (out_ref,), terms_ref, data, sems, lambda: None)


def partial_samples(data_slab, sketch_t):
    rows, columns = data_slab.shape
    quarter = rows // QUARTERS
    chunk = quarter // CHUNKS
    sample = jax.ShapeDtypeStruct((chunk, LANES), F32)

    def cost(count):
        return pl.CostEstimate(
            flops=8 * count * quarter * columns * K, bytes_accessed=4 * count * quarter * columns, transcendentals=0
        )

    def scratch(count):
        return [VMEM((count * CHUNKS, chunk, columns), F32)]

    *sent, sent_terms, weights = pl.pallas_call(
        send_kernel,
        out_shape=[sample] * len(SENT)
        + [
            jax.ShapeDtypeStruct((2 * len(SENT) * quarter, columns), BF16),
            jax.ShapeDtypeStruct((columns, LANES), BF16),
        ],
        in_specs=[pl.BlockSpec(memory_space=pltpu.HBM)] * 2,
        out_specs=vmem(len(SENT) + 2),
        scratch_shapes=scratch(len(SENT))
        + [VMEM((K, columns), F32), pltpu.SemaphoreType.DMA((len(SENT) * CHUNKS + 1,))],
        compiler_params=pltpu.CompilerParams(vmem_limit_bytes=42 * MIB),
        cost_estimate=cost(len(SENT)),
    )(in_hbm(data_slab), in_hbm(sketch_t))
    kept, kept_terms = pl.pallas_call(
        keep_kernel,
        out_shape=[sample, jax.ShapeDtypeStruct((2 * quarter, columns), BF16)],
        in_specs=[pl.BlockSpec(memory_space=pltpu.HBM)] + vmem(1),
        out_specs=vmem(2),
        scratch_shapes=scratch(1) + [pltpu.SemaphoreType.DMA((CHUNKS,))],
        compiler_params=pltpu.CompilerParams(vmem_limit_bytes=40 * MIB),
        cost_estimate=cost(1),
    )(in_hbm(data_slab), weights)
    return sent, sent_terms, kept, kept_terms


def left_of(sample):
    high, low = split(unpacked(sample).T)
    left = jnp.concatenate([high, low], axis=0)
    return left, jnp.concatenate([left, left], axis=1)


def term_kernel(sample_ref, terms_ref, *refs):
    out_ref = refs[-1]
    _, left = left_of(sample_ref[...])
    width = out_ref.shape[1] // GROUPS
    for g in range(GROUPS):
        at = pl.ds(g * width, width)
        total = jnp.dot(left, terms_ref[:, at], preferred_element_type=F32)
        total = total[:K] + total[K:]
        for ref in refs[:-1]:
            total += ref[:, at]
        out_ref[:, at] = total


def next_term_kernel(index, sample_ref, terms_ref, begun_ref, out_ref):
    size = terms_ref.shape[0] // len(SENT)
    term_kernel(sample_ref, terms_ref.at[pl.ds(index * size, size)], begun_ref, out_ref)


def half_blocks(first_group, index, sample_ref, terms_ref, begun_ref, out_ref):
    size = terms_ref.shape[0] // len(SENT)
    _, left = left_of(sample_ref[...])
    width = PER_GROUP * LANES
    for place, g in enumerate(ORDER):
        at = pl.ds(pl.multiple_of(group_place(first_group + g) * width, width), width)
        total = jnp.dot(left, terms_ref[pl.ds(index * size, size), at], preferred_element_type=F32)
        total = total[:K] + total[K:] + begun_ref[:, at]
        for t in range(PER_GROUP):
            out_ref[pl.ds((place * PER_GROUP + t) * K, K), :] = total[:, t * LANES : (t + 1) * LANES]


def sent_half_kernel(index, s0, s3, s2, s1, terms_ref, begun_ref, out_ref):
    every = jnp.concatenate([left_of(ref[...])[0] for ref in (s0, s3, s2, s1)], axis=1)
    gram = lax.dot_general(every, every, (((1,), (1,)), ((), ())), preferred_element_type=F32)
    gram = gram[:K] + gram[K:]
    gram = gram + pltpu.roll(gram, K, axis=1)
    lane = lax.broadcasted_iota(jnp.int32, (K // 2, LANES), 1)
    out_ref[BLOCKS // 2 * K :, :] = jnp.where(lane < K, gram[: K // 2], gram[K // 2 :])
    half_blocks(PER_GROUP, index, (s3, s2, s1)[index], terms_ref, begun_ref, out_ref)


def kept_half_kernel(index, sample_ref, terms_ref, begun_ref, sent_ref, out_ref):
    out_ref[BLOCKS // 2 * K :, :] = sent_ref[BLOCKS // 2 * K :, :]
    half_blocks(0, index, sample_ref, terms_ref, begun_ref, out_ref)


def term_cost(rows, columns):
    return pl.CostEstimate(flops=8 * K * rows * columns, bytes_accessed=4 * rows * columns, transcendentals=0)


def term_call(kernel, shape, operands, cost):
    return pl.pallas_call(
        kernel,
        out_shape=jax.ShapeDtypeStruct(shape, F32),
        in_specs=vmem(len(operands)),
        out_specs=vmem(1)[0],
        compiler_params=pltpu.CompilerParams(vmem_limit_bytes=16 * MIB),
        cost_estimate=cost,
    )(*operands)


def terms_of(quarters, kept_terms, sent_terms):
    size, columns = kept_terms.shape
    cost, less = term_cost(size // 2, columns), term_cost(size // 4, columns)
    whole = (K, columns)
    blocks = (BLOCKS // 2 * K + K // 2, LANES)
    begun = term_call(term_kernel, whole, (quarters[0], kept_terms), cost)
    for index in (0, 1):
        kernel = functools.partial(next_term_kernel, index)
        begun = term_call(kernel, whole, (quarters[1 + index], sent_terms, begun), cost)
    sent = term_call(functools.partial(sent_half_kernel, 2), blocks, (*quarters, sent_terms, begun), less)
    kernel = functools.partial(kept_half_kernel, 2)
    kept = term_call(kernel, blocks, (quarters[3], sent_terms, begun, sent), less)
    return kept, sent


def inverse_kernel(gram_ref, inverse_ref):
    lane = lax.broadcasted_iota(jnp.int32, (K // 2, LANES), 1)
    row = lax.broadcasted_iota(jnp.int32, (K // 2, LANES), 0)
    upper = gram_ref[...]
    lower = pltpu.roll(upper, K, axis=1)
    work = jnp.concatenate(
        [
            jnp.where(lane < K, upper, jnp.where(lane == row + K, 1.0, 0.0)),
            jnp.where(lane < K, lower, jnp.where(lane == row + K + K // 2, 1.0, 0.0)),
        ],
        axis=0,
    )
    count = K // 8
    parts = [work[8 * i : 8 * i + 8] for i in range(count)]
    sub = lax.broadcasted_iota(jnp.int32, (8, LANES), 0)
    diagonal = [jnp.ones((8, LANES), F32)] * count

    def full(value):
        return jnp.broadcast_to(value, (8, LANES))

    for j in range(0, K, 4):
        block, at = divmod(j, 8)
        own = parts[block]
        c1, c2, c3, c4 = [[full(parts[i][:, j + c : j + c + 1]) for i in range(block, count)] for c in range(4)]
        r1, r2, r3, r4 = [full(own[at + r : at + r + 1]) for r in range(4)]
        a11, a12, a13, a14 = [full(c[0][at : at + 1]) for c in (c1, c2, c3, c4)]
        a22, a23, a24 = [full(c[0][at + 1 : at + 2]) for c in (c2, c3, c4)]
        a33, a34 = [full(c[0][at + 2 : at + 3]) for c in (c3, c4)]
        a44 = full(c4[0][at + 3 : at + 4])
        first = a11 * a22 - a12 * a12
        scale = 1.0 / first
        l31, l32 = (a22 * a13 - a12 * a23) * scale, (a11 * a23 - a12 * a13) * scale
        l41, l42 = (a22 * a14 - a12 * a24) * scale, (a11 * a24 - a12 * a14) * scale
        s33 = a33 - (l31 * a13 + l32 * a23)
        s34 = a34 - (l31 * a14 + l32 * a24)
        s44 = a44 - (l41 * a14 + l42 * a24)
        r3 = r3 - (l31 * r1 + l32 * r2)
        r4 = r4 - (l41 * r1 + l42 * r2)
        second = s33 * s44 - s34 * s34
        again = 1.0 / second
        v1, v2 = (a22 * r1 - a12 * r2) * scale, (a11 * r2 - a12 * r1) * scale
        v3, v4 = (s44 * r3 - s34 * r4) * again, (s33 * r4 - s34 * r3) * again
        p1, p3 = 1.0 / a11, 1.0 / s33
        rows = (r2 - a12 * p1 * r1, r3, r4 - s34 * p3 * r3)
        diag = (a11, first * p1, s33, second * p3)
        for r in range(4):
            diagonal[block] = jnp.where(sub == at + r, diag[r], diagonal[block])
        for i in range(block, count):
            f1, f2, f3, f4 = [c[i - block] for c in (c1, c2, c3, c4)]
            f3 = f3 - (f1 * l31 + f2 * l32)
            f4 = f4 - (f1 * l41 + f2 * l42)
            new = parts[i] - ((f1 * v1 + f2 * v2) + (f3 * v3 + f4 * v4))
            if i == block:
                new = jnp.where(sub > at + 3, new, own)
                for r in range(3):
                    new = jnp.where(sub == at + 1 + r, rows[r], new)
            parts[i] = new
    parts = [part * (1.0 / jnp.sqrt(diag)) for part, diag in zip(parts, diagonal)]
    inverse_ref[...] = jnp.concatenate(parts, axis=0)[:, K:]


def inverse_of(gram):
    return pl.pallas_call(
        inverse_kernel,
        out_shape=jax.ShapeDtypeStruct((K, K), F32),
        in_specs=vmem(1),
        out_specs=vmem(1)[0],
        compiler_params=pltpu.CompilerParams(vmem_limit_bytes=8 * MIB),
        cost_estimate=pl.CostEstimate(flops=K**3 * 100, bytes_accessed=8 * K * K, transcendentals=K),
    )(gram)


def basis_kernel(scale, inverse_ref, s0, s3, s2, s1, basis_ref, sample):
    half = s0.shape[0]
    mine = own_quarter()
    for mask, ref in ((0, s0), (3, s3), (2, s2), (1, s1)):
        start = pl.multiple_of((mine ^ mask) * 2 * half, 2 * half)
        sample[pl.ds(start, half), :] = ref[:, :K]
        sample[pl.ds(start + half, half), :] = ref[:, K:]
    basis_ref[...] = lax.dot_general(
        inverse_ref[...] * scale,
        sample[...],
        (((1,), (1,)), ((), ())),
        precision=lax.Precision.HIGHEST,
        preferred_element_type=F32,
    )


def basis_of(inverse, quarters, rows, scale):
    return pl.pallas_call(
        functools.partial(basis_kernel, scale),
        out_shape=jax.ShapeDtypeStruct((K, rows), F32),
        in_specs=vmem(1 + len(quarters)),
        out_specs=vmem(1)[0],
        scratch_shapes=[VMEM((rows, K), F32)],
        compiler_params=pltpu.CompilerParams(vmem_limit_bytes=8 * MIB),
        cost_estimate=pl.CostEstimate(flops=12 * rows * K * K, bytes_accessed=8 * rows * K, transcendentals=0),
    )(inverse, *quarters)


def apply_kernel(first_group, inverse_ref, value_ref, *refs):
    out_ref, parts, sems = refs[-3:]
    high, low = split(inverse_ref[...])
    left = jnp.concatenate([high, low, high], axis=1)
    width = PER_GROUP * LANES
    copies = []
    for g in range(PER_GROUP):
        rows = [value_ref[pl.ds((g * PER_GROUP + t) * K, K), :] for t in range(PER_GROUP)]
        high, low = split(jnp.concatenate(rows, axis=1))
        right = jnp.concatenate([high, high, low], axis=0)
        parts[g] = jnp.dot(left, right, preferred_element_type=F32)
        at = pl.ds(pl.multiple_of(group_place(first_group + g) * width, width), width)
        copies.append(pltpu.make_async_copy(parts.at[g], out_ref.at[:, at], sems.at[g]))
        copies[g].start()
    for copy in copies:
        copy.wait()


def applied(first_group, inverse, value, begun=None):
    columns = BLOCKS * LANES
    more = [] if begun is None else [begun]
    return pl.pallas_call(
        functools.partial(apply_kernel, first_group),
        out_shape=jax.ShapeDtypeStruct((K, columns), F32),
        in_specs=vmem(2) + [pl.BlockSpec(memory_space=pl.ANY)] * len(more),
        out_specs=pl.BlockSpec(memory_space=pl.ANY),
        input_output_aliases={2: 0} if more else {},
        scratch_shapes=[VMEM((PER_GROUP, K, PER_GROUP * LANES), F32), pltpu.SemaphoreType.DMA((PER_GROUP,))],
        compiler_params=pltpu.CompilerParams(vmem_limit_bytes=8 * MIB),
        cost_estimate=pl.CostEstimate(flops=3 * columns * K * K, bytes_accessed=4 * columns * K, transcendentals=0),
    )(inverse, value, *more)


def along_col(value, mask):
    return lax.ppermute(value, "col", [(i, i ^ mask) for i in range(8)])


def along_row(value, masks):
    return lax.ppermute(value, "row", [(i, i ^ masks[i % 2]) for i in range(32)])


CORE = (1, 1)
FIRST = [(t << 3, t << 1) for t in range(4)]
SECOND = [(t << 1, t << 3) for t in range(4)]


def body(data_slab, sketch):
    rows = data_slab.shape[0]
    sent, sent_terms, kept, kept_terms = partial_samples(data_slab, sketch.T)
    got = [along_col(part, mask) for part, mask in zip(sent, SENT)]
    own = kept + got[0] + got[1] + got[2]
    own = own + along_col(own, 7)
    quarters = [own] + [along_col(own, mask) for mask in SENT]

    keep, send = terms_of(quarters, kept_terms, sent_terms)
    total = keep + along_row(send, CORE)
    size = PER_GROUP * K
    gram = total[4 * size :]
    places = {t: ORDER.index(t) * size for t in (3, 1, 2)}
    got = [along_row(jnp.concatenate([total[p : p + size], gram]), FIRST[t]) for t, p in places.items()]
    total = jnp.concatenate([total[:size], gram]) + got[0] + got[1] + got[2]
    got = [along_row(total, SECOND[t]) for t in (1, 3, 2)]
    total = total + got[0] + got[1] + got[2]

    inverse = inverse_of(total[size:])
    block = total[:size]
    mine = jnp.concatenate([block] + [along_row(block, FIRST[t]) for t in (1, 2, 3)])
    range_basis = basis_of(inverse, quarters, rows, math.sqrt(rows * lax.axis_size("row")))
    mine, inverse, range_basis = lax.optimization_barrier((mine, inverse, range_basis))
    theirs = along_row(mine, CORE)
    projected = applied(PER_GROUP, inverse, theirs, applied(0, inverse, mine))
    return range_basis.T, projected


def solution(mesh):
    placed = (P("row", "col"), P("col", None))
    return jax.shard_map(
        body,
        mesh=mesh,
        in_specs=placed,
        out_specs=(P("row", None), P(None, "col")),
        check_vma=False,
    )
```

```python
import functools
import math

import jax
import jax.numpy as jnp
from jax import lax
from jax.experimental import pallas as pl
from jax.experimental.pallas import tpu as pltpu
from jax.sharding import PartitionSpec as P

F32 = jnp.float32
BF16 = jnp.bfloat16
VMEM = pltpu.VMEM
MIB = 2**20
K = 64
LANES = 128
QUARTERS = 4
CHUNKS = 2
BLOCKS = 32
GROUPS = 8
PER_GROUP = 4


def split(value):
    high = value.astype(BF16)
    return high, (value - high.astype(F32)).astype(BF16)


def own_quarter():
    z = lax.axis_index("col")
    return jnp.where(z < QUARTERS, z, 2 * QUARTERS - 1 - z)


def position():
    row = lax.axis_index("row")
    core, y, x = row % 2, (row // 2) % 4, row // 8
    return core, jnp.where(core == 0, x, y), jnp.where(core == 0, y, x)


def group_place(group):
    core, first, second = position()
    if group < PER_GROUP:
        return core * PER_GROUP + (first ^ group)
    return (1 - core) * PER_GROUP + (second ^ (group - PER_GROUP))


def in_hbm(value):
    return pltpu.with_memory_space_constraint(value, pltpu.HBM)


def vmem(count):
    return [pl.BlockSpec(memory_space=VMEM)] * count


def unpacked(value):
    return jnp.concatenate([value[:, :K], value[:, K:]], axis=0)


def sample_quarters(data_ref, masks, weights, outs, terms_ref, data, sems, prepare):
    chunk = data.shape[1]
    rows = CHUNKS * chunk
    mine = own_quarter()
    copies = []
    for i in range(len(masks) * CHUNKS):
        start = pl.multiple_of((mine ^ masks[i // CHUNKS]) * rows + i % CHUNKS * chunk, chunk)
        copies.append(pltpu.make_async_copy(data_ref.at[pl.ds(start, chunk)], data.at[i], sems.at[i]))
        copies[i].start()
    prepare()
    lane = lax.broadcasted_iota(jnp.int32, (chunk, LANES), 1)
    for q in range(len(masks)):
        totals = []
        for i in range(CHUNKS):
            at = q * CHUNKS + i
            copies[at].wait()
            high, low = split(data[at])
            terms_ref[pl.ds(2 * q * rows + i * chunk, chunk), :] = high
            terms_ref[pl.ds((2 * q + 1) * rows + i * chunk, chunk), :] = low
            total = jnp.dot(jnp.concatenate([high, low], axis=0), weights[...], preferred_element_type=F32)
            total = total[:chunk] + total[chunk:]
            totals.append(total + pltpu.roll(total, K, axis=1))
        half = CHUNKS // 2
        for i in range(half):
            outs[q][pl.ds(i * chunk, chunk), :] = jnp.where(lane < K, totals[i], totals[i + half])


SENT = (3, 2, 1)
ORDER = (0, 1, 3, 2)


def send_kernel(data_ref, sketch_ref, out3, out2, out1, terms_ref, weights_ref, data, sketch, sems):
    load = pltpu.make_async_copy(sketch_ref, sketch, sems.at[len(SENT) * CHUNKS])
    load.start()

    def prepare():
        load.wait()
        high, low = split(sketch[...])
        both = jnp.concatenate([high.astype(F32), low.astype(F32)], axis=0)
        weights_ref[...] = both.T.astype(BF16)

    sample_quarters(data_ref, SENT, weights_ref, (out3, out2, out1), terms_ref, data, sems, prepare)


def keep_kernel(data_ref, weights_ref, out_ref, terms_ref, data, sems):
    sample_quarters(data_ref, (0,), weights_ref, (out_ref,), terms_ref, data, sems, lambda: None)


def partial_samples(data_slab, sketch_t):
    rows, columns = data_slab.shape
    quarter = rows // QUARTERS
    chunk = quarter // CHUNKS
    sample = jax.ShapeDtypeStruct((chunk, LANES), F32)

    def cost(count):
        return pl.CostEstimate(
            flops=8 * count * quarter * columns * K, bytes_accessed=4 * count * quarter * columns, transcendentals=0
        )

    def scratch(count):
        return [VMEM((count * CHUNKS, chunk, columns), F32)]

    *sent, sent_terms, weights = pl.pallas_call(
        send_kernel,
        out_shape=[sample] * len(SENT)
        + [
            jax.ShapeDtypeStruct((2 * len(SENT) * quarter, columns), BF16),
            jax.ShapeDtypeStruct((columns, LANES), BF16),
        ],
        in_specs=[pl.BlockSpec(memory_space=pltpu.HBM)] * 2,
        out_specs=vmem(len(SENT) + 2),
        scratch_shapes=scratch(len(SENT))
        + [VMEM((K, columns), F32), pltpu.SemaphoreType.DMA((len(SENT) * CHUNKS + 1,))],
        compiler_params=pltpu.CompilerParams(vmem_limit_bytes=42 * MIB),
        cost_estimate=cost(len(SENT)),
    )(in_hbm(data_slab), in_hbm(sketch_t))
    kept, kept_terms = pl.pallas_call(
        keep_kernel,
        out_shape=[sample, jax.ShapeDtypeStruct((2 * quarter, columns), BF16)],
        in_specs=[pl.BlockSpec(memory_space=pltpu.HBM)] + vmem(1),
        out_specs=vmem(2),
        scratch_shapes=scratch(1) + [pltpu.SemaphoreType.DMA((CHUNKS,))],
        compiler_params=pltpu.CompilerParams(vmem_limit_bytes=40 * MIB),
        cost_estimate=cost(1),
    )(in_hbm(data_slab), weights)
    return sent, sent_terms, kept, kept_terms


def left_of(sample):
    high, low = split(unpacked(sample).T)
    left = jnp.concatenate([high, low], axis=0)
    return left, jnp.concatenate([left, left], axis=1)


def term_kernel(sample_ref, terms_ref, *refs):
    out_ref = refs[-1]
    _, left = left_of(sample_ref[...])
    width = out_ref.shape[1] // GROUPS
    for g in range(GROUPS):
        at = pl.ds(g * width, width)
        total = jnp.dot(left, terms_ref[:, at], preferred_element_type=F32)
        total = total[:K] + total[K:]
        for ref in refs[:-1]:
            total += ref[:, at]
        out_ref[:, at] = total


def next_term_kernel(index, sample_ref, terms_ref, begun_ref, out_ref):
    size = terms_ref.shape[0] // len(SENT)
    term_kernel(sample_ref, terms_ref.at[pl.ds(index * size, size)], begun_ref, out_ref)


def half_blocks(first_group, index, sample_ref, terms_ref, begun_ref, out_ref):
    size = terms_ref.shape[0] // len(SENT)
    _, left = left_of(sample_ref[...])
    width = PER_GROUP * LANES
    for place, g in enumerate(ORDER):
        at = pl.ds(pl.multiple_of(group_place(first_group + g) * width, width), width)
        total = jnp.dot(left, terms_ref[pl.ds(index * size, size), at], preferred_element_type=F32)
        total = total[:K] + total[K:] + begun_ref[:, at]
        for t in range(PER_GROUP):
            out_ref[pl.ds((place * PER_GROUP + t) * K, K), :] = total[:, t * LANES : (t + 1) * LANES]


def sent_half_kernel(index, s0, s3, s2, s1, terms_ref, begun_ref, out_ref):
    every = jnp.concatenate([left_of(ref[...])[0] for ref in (s0, s3, s2, s1)], axis=1)
    gram = lax.dot_general(every, every, (((1,), (1,)), ((), ())), preferred_element_type=F32)
    gram = gram[:K] + gram[K:]
    gram = gram + pltpu.roll(gram, K, axis=1)
    lane = lax.broadcasted_iota(jnp.int32, (K // 2, LANES), 1)
    out_ref[BLOCKS // 2 * K :, :] = jnp.where(lane < K, gram[: K // 2], gram[K // 2 :])
    half_blocks(PER_GROUP, index, (s3, s2, s1)[index], terms_ref, begun_ref, out_ref)


def kept_half_kernel(index, sample_ref, terms_ref, begun_ref, sent_ref, out_ref):
    out_ref[BLOCKS // 2 * K :, :] = sent_ref[BLOCKS // 2 * K :, :]
    half_blocks(0, index, sample_ref, terms_ref, begun_ref, out_ref)


def term_cost(rows, columns):
    return pl.CostEstimate(flops=8 * K * rows * columns, bytes_accessed=4 * rows * columns, transcendentals=0)


def term_call(kernel, shape, operands, cost):
    return pl.pallas_call(
        kernel,
        out_shape=jax.ShapeDtypeStruct(shape, F32),
        in_specs=vmem(len(operands)),
        out_specs=vmem(1)[0],
        compiler_params=pltpu.CompilerParams(vmem_limit_bytes=16 * MIB),
        cost_estimate=cost,
    )(*operands)


def terms_of(quarters, kept_terms, sent_terms):
    size, columns = kept_terms.shape
    cost, less = term_cost(size // 2, columns), term_cost(size // 4, columns)
    whole = (K, columns)
    blocks = (BLOCKS // 2 * K + K // 2, LANES)
    begun = term_call(term_kernel, whole, (quarters[0], kept_terms), cost)
    for index in (0, 1):
        kernel = functools.partial(next_term_kernel, index)
        begun = term_call(kernel, whole, (quarters[1 + index], sent_terms, begun), cost)
    sent = term_call(functools.partial(sent_half_kernel, 2), blocks, (*quarters, sent_terms, begun), less)
    kernel = functools.partial(kept_half_kernel, 2)
    kept = term_call(kernel, blocks, (quarters[3], sent_terms, begun, sent), less)
    return kept, sent


def inverse_kernel(gram_ref, inverse_ref):
    lane = lax.broadcasted_iota(jnp.int32, (K // 2, LANES), 1)
    row = lax.broadcasted_iota(jnp.int32, (K // 2, LANES), 0)
    upper = gram_ref[...]
    lower = pltpu.roll(upper, K, axis=1)
    work = jnp.concatenate(
        [
            jnp.where(lane < K, upper, jnp.where(lane == row + K, 1.0, 0.0)),
            jnp.where(lane < K, lower, jnp.where(lane == row + K + K // 2, 1.0, 0.0)),
        ],
        axis=0,
    )
    lane = lax.broadcasted_iota(jnp.int32, (K, LANES), 1)
    own = jnp.where(lane == lax.broadcasted_iota(jnp.int32, (K, LANES), 0), work, 0.0)
    column = 1.0 / jnp.sqrt(jnp.sum(own, axis=1, keepdims=True))
    line = jnp.where(lane[:1] < K, 1.0 / jnp.sqrt(jnp.sum(own, axis=0, keepdims=True)), 1.0)
    work = work * column * line
    count = K // 8
    parts = [work[8 * i : 8 * i + 8] for i in range(count)]
    sub = lax.broadcasted_iota(jnp.int32, (8, LANES), 0)
    diagonal = [jnp.ones((8, LANES), F32)] * count

    def full(value):
        return jnp.broadcast_to(value, (8, LANES))

    for j in range(0, K, 4):
        block, at = divmod(j, 8)
        own = parts[block]
        c1, c2, c3, c4 = [[full(parts[i][:, j + c : j + c + 1]) for i in range(block, count)] for c in range(4)]
        r1, r2, r3, r4 = [full(own[at + r : at + r + 1]) for r in range(4)]
        a11, a12, a13, a14 = [full(c[0][at : at + 1]) for c in (c1, c2, c3, c4)]
        a22, a23, a24 = [full(c[0][at + 1 : at + 2]) for c in (c2, c3, c4)]
        a33, a34 = [full(c[0][at + 2 : at + 3]) for c in (c3, c4)]
        a44 = full(c4[0][at + 3 : at + 4])
        first = a11 * a22 - a12 * a12
        scale = 1.0 / first
        l31, l32 = (a22 * a13 - a12 * a23) * scale, (a11 * a23 - a12 * a13) * scale
        l41, l42 = (a22 * a14 - a12 * a24) * scale, (a11 * a24 - a12 * a14) * scale
        s33 = a33 - (l31 * a13 + l32 * a23)
        s34 = a34 - (l31 * a14 + l32 * a24)
        s44 = a44 - (l41 * a14 + l42 * a24)
        r3 = r3 - (l31 * r1 + l32 * r2)
        r4 = r4 - (l41 * r1 + l42 * r2)
        second = s33 * s44 - s34 * s34
        again = 1.0 / second
        v1, v2 = (a22 * r1 - a12 * r2) * scale, (a11 * r2 - a12 * r1) * scale
        v3, v4 = (s44 * r3 - s34 * r4) * again, (s33 * r4 - s34 * r3) * again
        p1, p3 = 1.0 / a11, 1.0 / s33
        rows = (r2 - a12 * p1 * r1, r3, r4 - s34 * p3 * r3)
        diag = (a11, first * p1, s33, second * p3)
        for r in range(4):
            diagonal[block] = jnp.where(sub == at + r, diag[r], diagonal[block])
        for i in range(block, count):
            f1, f2, f3, f4 = [c[i - block] for c in (c1, c2, c3, c4)]
            f3 = f3 - (f1 * l31 + f2 * l32)
            f4 = f4 - (f1 * l41 + f2 * l42)
            new = parts[i] - ((f1 * v1 + f2 * v2) + (f3 * v3 + f4 * v4))
            if i == block:
                new = jnp.where(sub > at + 3, new, own)
                for r in range(3):
                    new = jnp.where(sub == at + 1 + r, rows[r], new)
            parts[i] = new
    parts = [part * (1.0 / jnp.sqrt(diag)) for part, diag in zip(parts, diagonal)]
    inverse_ref[...] = jnp.concatenate(parts, axis=0)[:, K:]


def inverse_of(gram):
    return pl.pallas_call(
        inverse_kernel,
        out_shape=jax.ShapeDtypeStruct((K, K), F32),
        in_specs=vmem(1),
        out_specs=vmem(1)[0],
        compiler_params=pltpu.CompilerParams(vmem_limit_bytes=8 * MIB),
        cost_estimate=pl.CostEstimate(flops=K**3 * 100, bytes_accessed=8 * K * K, transcendentals=K),
    )(gram)


def basis_kernel(scale, inverse_ref, s0, s3, s2, s1, basis_ref, sample):
    half = s0.shape[0]
    mine = own_quarter()
    for mask, ref in ((0, s0), (3, s3), (2, s2), (1, s1)):
        start = pl.multiple_of((mine ^ mask) * 2 * half, 2 * half)
        sample[pl.ds(start, half), :] = ref[:, :K]
        sample[pl.ds(start + half, half), :] = ref[:, K:]
    basis_ref[...] = lax.dot_general(
        inverse_ref[...] * scale,
        sample[...],
        (((1,), (1,)), ((), ())),
        precision=lax.Precision.HIGHEST,
        preferred_element_type=F32,
    )


def basis_of(inverse, quarters, rows, scale):
    return pl.pallas_call(
        functools.partial(basis_kernel, scale),
        out_shape=jax.ShapeDtypeStruct((K, rows), F32),
        in_specs=vmem(1 + len(quarters)),
        out_specs=vmem(1)[0],
        scratch_shapes=[VMEM((rows, K), F32)],
        compiler_params=pltpu.CompilerParams(vmem_limit_bytes=8 * MIB),
        cost_estimate=pl.CostEstimate(flops=12 * rows * K * K, bytes_accessed=8 * rows * K, transcendentals=0),
    )(inverse, *quarters)


def apply_kernel(first_group, inverse_ref, value_ref, *refs):
    out_ref, parts, sems = refs[-3:]
    high, low = split(inverse_ref[...])
    left = jnp.concatenate([high, low, high], axis=1)
    width = PER_GROUP * LANES
    copies = []
    for g in range(PER_GROUP):
        rows = [value_ref[pl.ds((g * PER_GROUP + t) * K, K), :] for t in range(PER_GROUP)]
        high, low = split(jnp.concatenate(rows, axis=1))
        right = jnp.concatenate([high, high, low], axis=0)
        parts[g] = jnp.dot(left, right, preferred_element_type=F32)
        at = pl.ds(pl.multiple_of(group_place(first_group + g) * width, width), width)
        copies.append(pltpu.make_async_copy(parts.at[g], out_ref.at[:, at], sems.at[g]))
        copies[g].start()
    for copy in copies:
        copy.wait()


def applied(first_group, inverse, value, begun=None):
    columns = BLOCKS * LANES
    more = [] if begun is None else [begun]
    return pl.pallas_call(
        functools.partial(apply_kernel, first_group),
        out_shape=jax.ShapeDtypeStruct((K, columns), F32),
        in_specs=vmem(2) + [pl.BlockSpec(memory_space=pl.ANY)] * len(more),
        out_specs=pl.BlockSpec(memory_space=pl.ANY),
        input_output_aliases={2: 0} if more else {},
        scratch_shapes=[VMEM((PER_GROUP, K, PER_GROUP * LANES), F32), pltpu.SemaphoreType.DMA((PER_GROUP,))],
        compiler_params=pltpu.CompilerParams(vmem_limit_bytes=8 * MIB),
        cost_estimate=pl.CostEstimate(flops=3 * columns * K * K, bytes_accessed=4 * columns * K, transcendentals=0),
    )(inverse, value, *more)


def along_col(value, mask):
    return lax.ppermute(value, "col", [(i, i ^ mask) for i in range(8)])


def along_row(value, masks):
    return lax.ppermute(value, "row", [(i, i ^ masks[i % 2]) for i in range(32)])


CORE = (1, 1)
FIRST = [(t << 3, t << 1) for t in range(4)]
SECOND = [(t << 1, t << 3) for t in range(4)]


def body(data_slab, sketch):
    rows = data_slab.shape[0]
    sent, sent_terms, kept, kept_terms = partial_samples(data_slab, sketch.T)
    got = [along_col(part, mask) for part, mask in zip(sent, SENT)]
    own = kept + got[0] + got[1] + got[2]
    own = own + along_col(own, 7)
    quarters = [own] + [along_col(own, mask) for mask in SENT]

    keep, send = terms_of(quarters, kept_terms, sent_terms)
    total = keep + along_row(send, CORE)
    size = PER_GROUP * K
    gram = total[4 * size :]
    places = {t: ORDER.index(t) * size for t in (3, 1, 2)}
    got = [along_row(jnp.concatenate([total[p : p + size], gram]), FIRST[t]) for t, p in places.items()]
    total = jnp.concatenate([total[:size], gram]) + got[0] + got[1] + got[2]
    got = [along_row(total, SECOND[t]) for t in (1, 3, 2)]
    total = total + got[0] + got[1] + got[2]

    inverse = inverse_of(total[size:])
    block = total[:size]
    mine = jnp.concatenate([block] + [along_row(block, FIRST[t]) for t in (1, 2, 3)])
    range_basis = basis_of(inverse, quarters, rows, math.sqrt(rows * lax.axis_size("row")))
    mine, inverse, range_basis = lax.optimization_barrier((mine, inverse, range_basis))
    theirs = along_row(mine, CORE)
    projected = applied(PER_GROUP, inverse, theirs, applied(0, inverse, mine))
    return range_basis.T, projected


def solution(mesh):
    placed = (P("row", "col"), P("col", None))
    return jax.shard_map(
        body,
        mesh=mesh,
        in_specs=placed,
        out_specs=(P("row", None), P(None, "col")),
        check_vma=False,
    )
```

```python
import functools
import math

import jax
import jax.numpy as jnp
from jax import lax
from jax.experimental import pallas as pl
from jax.experimental.pallas import tpu as pltpu
from jax.sharding import PartitionSpec as P

F32 = jnp.float32
BF16 = jnp.bfloat16
VMEM = pltpu.VMEM
MIB = 2**20
K = 64
LANES = 128
QUARTERS = 4
CHUNKS = 2
BLOCKS = 32
GROUPS = 8
PER_GROUP = 4


def split(value):
    high = value.astype(BF16)
    return high, (value - high.astype(F32)).astype(BF16)


def own_quarter():
    z = lax.axis_index("col")
    return jnp.where(z < QUARTERS, z, 2 * QUARTERS - 1 - z)


def position():
    row = lax.axis_index("row")
    core, y, x = row % 2, (row // 2) % 4, row // 8
    return core, jnp.where(core == 0, x, y), jnp.where(core == 0, y, x)


def group_place(group):
    core, first, second = position()
    if group < PER_GROUP:
        return core * PER_GROUP + (first ^ group)
    return (1 - core) * PER_GROUP + (second ^ (group - PER_GROUP))


def in_hbm(value):
    return pltpu.with_memory_space_constraint(value, pltpu.HBM)


def vmem(count):
    return [pl.BlockSpec(memory_space=VMEM)] * count


def unpacked(value):
    return jnp.concatenate([value[:, :K], value[:, K:]], axis=0)


def sample_quarters(data_ref, masks, weights, outs, terms_ref, data, sems, prepare):
    chunk = data.shape[1]
    rows = CHUNKS * chunk
    mine = own_quarter()
    copies = []
    for i in range(len(masks) * CHUNKS):
        start = pl.multiple_of((mine ^ masks[i // CHUNKS]) * rows + i % CHUNKS * chunk, chunk)
        copies.append(pltpu.make_async_copy(data_ref.at[pl.ds(start, chunk)], data.at[i], sems.at[i]))
        copies[i].start()
    prepare()
    lane = lax.broadcasted_iota(jnp.int32, (chunk, LANES), 1)
    for q in range(len(masks)):
        totals = []
        for i in range(CHUNKS):
            at = q * CHUNKS + i
            copies[at].wait()
            high, low = split(data[at])
            terms_ref[pl.ds(2 * q * rows + i * chunk, chunk), :] = high
            terms_ref[pl.ds((2 * q + 1) * rows + i * chunk, chunk), :] = low
            total = jnp.dot(jnp.concatenate([high, low], axis=0), weights[...], preferred_element_type=F32)
            total = total[:chunk] + total[chunk:]
            totals.append(total + pltpu.roll(total, K, axis=1))
        half = CHUNKS // 2
        for i in range(half):
            outs[q][pl.ds(i * chunk, chunk), :] = jnp.where(lane < K, totals[i], totals[i + half])


SENT = (3, 2, 1)
ORDER = (0, 1, 3, 2)


def send_kernel(data_ref, sketch_ref, out3, out2, out1, terms_ref, weights_ref, data, sketch, sems):
    load = pltpu.make_async_copy(sketch_ref, sketch, sems.at[len(SENT) * CHUNKS])
    load.start()

    def prepare():
        load.wait()
        high, low = split(sketch[...])
        both = jnp.concatenate([high.astype(F32), low.astype(F32)], axis=0)
        weights_ref[...] = both.T.astype(BF16)

    sample_quarters(data_ref, SENT, weights_ref, (out3, out2, out1), terms_ref, data, sems, prepare)


def keep_kernel(data_ref, weights_ref, out_ref, terms_ref, data, sems):
    sample_quarters(data_ref, (0,), weights_ref, (out_ref,), terms_ref, data, sems, lambda: None)


def partial_samples(data_slab, sketch_t):
    rows, columns = data_slab.shape
    quarter = rows // QUARTERS
    chunk = quarter // CHUNKS
    sample = jax.ShapeDtypeStruct((chunk, LANES), F32)

    def cost(count):
        return pl.CostEstimate(
            flops=8 * count * quarter * columns * K, bytes_accessed=4 * count * quarter * columns, transcendentals=0
        )

    def scratch(count):
        return [VMEM((count * CHUNKS, chunk, columns), F32)]

    *sent, sent_terms, weights = pl.pallas_call(
        send_kernel,
        out_shape=[sample] * len(SENT)
        + [
            jax.ShapeDtypeStruct((2 * len(SENT) * quarter, columns), BF16),
            jax.ShapeDtypeStruct((columns, LANES), BF16),
        ],
        in_specs=[pl.BlockSpec(memory_space=pltpu.HBM)] * 2,
        out_specs=vmem(len(SENT) + 2),
        scratch_shapes=scratch(len(SENT))
        + [VMEM((K, columns), F32), pltpu.SemaphoreType.DMA((len(SENT) * CHUNKS + 1,))],
        compiler_params=pltpu.CompilerParams(vmem_limit_bytes=42 * MIB),
        cost_estimate=cost(len(SENT)),
    )(in_hbm(data_slab), in_hbm(sketch_t))
    kept, kept_terms = pl.pallas_call(
        keep_kernel,
        out_shape=[sample, jax.ShapeDtypeStruct((2 * quarter, columns), BF16)],
        in_specs=[pl.BlockSpec(memory_space=pltpu.HBM)] + vmem(1),
        out_specs=vmem(2),
        scratch_shapes=scratch(1) + [pltpu.SemaphoreType.DMA((CHUNKS,))],
        compiler_params=pltpu.CompilerParams(vmem_limit_bytes=40 * MIB),
        cost_estimate=cost(1),
    )(in_hbm(data_slab), weights)
    return sent, sent_terms, kept, kept_terms


def left_of(sample):
    high, low = split(unpacked(sample).T)
    left = jnp.concatenate([high, low], axis=0)
    return left, jnp.concatenate([left, left], axis=1)


def term_kernel(sample_ref, terms_ref, *refs):
    out_ref = refs[-1]
    _, left = left_of(sample_ref[...])
    width = out_ref.shape[1] // GROUPS
    for g in range(GROUPS):
        at = pl.ds(g * width, width)
        total = jnp.dot(left, terms_ref[:, at], preferred_element_type=F32)
        total = total[:K] + total[K:]
        for ref in refs[:-1]:
            total += ref[:, at]
        out_ref[:, at] = total


def next_term_kernel(index, sample_ref, terms_ref, begun_ref, out_ref):
    size = terms_ref.shape[0] // len(SENT)
    term_kernel(sample_ref, terms_ref.at[pl.ds(index * size, size)], begun_ref, out_ref)


def half_blocks(first_group, index, sample_ref, terms_ref, begun_ref, out_ref):
    size = terms_ref.shape[0] // len(SENT)
    _, left = left_of(sample_ref[...])
    width = PER_GROUP * LANES
    for place, g in enumerate(ORDER):
        at = pl.ds(pl.multiple_of(group_place(first_group + g) * width, width), width)
        total = jnp.dot(left, terms_ref[pl.ds(index * size, size), at], preferred_element_type=F32)
        total = total[:K] + total[K:] + begun_ref[:, at]
        for t in range(PER_GROUP):
            out_ref[pl.ds((place * PER_GROUP + t) * K, K), :] = total[:, t * LANES : (t + 1) * LANES]


def sent_half_kernel(index, s0, s3, s2, s1, terms_ref, begun_ref, out_ref):
    every = jnp.concatenate([ref[...] for ref in (s0, s3, s2, s1)], axis=0).T
    both = jnp.concatenate(split(every), axis=0)
    gram = lax.dot_general(both, both, (((1,), (1,)), ((), ())), preferred_element_type=F32)
    gram = gram[:LANES] + gram[LANES:]
    gram = gram[:, :LANES] + gram[:, LANES:]
    gram = gram[:K] + pltpu.roll(gram[K:], K, axis=1)
    lane = lax.broadcasted_iota(jnp.int32, (K // 2, LANES), 1)
    turned = pltpu.roll(gram[K // 2 :], K, axis=1)
    out_ref[BLOCKS // 2 * K :, :] = jnp.where(lane < K, gram[: K // 2], turned)
    half_blocks(PER_GROUP, index, (s3, s2, s1)[index], terms_ref, begun_ref, out_ref)


def kept_half_kernel(index, sample_ref, terms_ref, begun_ref, sent_ref, out_ref):
    out_ref[BLOCKS // 2 * K :, :] = sent_ref[BLOCKS // 2 * K :, :]
    half_blocks(0, index, sample_ref, terms_ref, begun_ref, out_ref)


def term_cost(rows, columns):
    return pl.CostEstimate(flops=8 * K * rows * columns, bytes_accessed=4 * rows * columns, transcendentals=0)


def term_call(kernel, shape, operands, cost):
    return pl.pallas_call(
        kernel,
        out_shape=jax.ShapeDtypeStruct(shape, F32),
        in_specs=vmem(len(operands)),
        out_specs=vmem(1)[0],
        compiler_params=pltpu.CompilerParams(vmem_limit_bytes=16 * MIB),
        cost_estimate=cost,
    )(*operands)


def terms_of(quarters, kept_terms, sent_terms):
    size, columns = kept_terms.shape
    cost, less = term_cost(size // 2, columns), term_cost(size // 4, columns)
    whole = (K, columns)
    blocks = (BLOCKS // 2 * K + K // 2, LANES)
    begun = term_call(term_kernel, whole, (quarters[0], kept_terms), cost)
    for index in (0, 1):
        kernel = functools.partial(next_term_kernel, index)
        begun = term_call(kernel, whole, (quarters[1 + index], sent_terms, begun), cost)
    sent = term_call(functools.partial(sent_half_kernel, 2), blocks, (*quarters, sent_terms, begun), less)
    kernel = functools.partial(kept_half_kernel, 2)
    kept = term_call(kernel, blocks, (quarters[3], sent_terms, begun, sent), less)
    return kept, sent


def inverse_kernel(gram_ref, inverse_ref):
    lane = lax.broadcasted_iota(jnp.int32, (K // 2, LANES), 1)
    row = lax.broadcasted_iota(jnp.int32, (K // 2, LANES), 0)
    upper = gram_ref[...]
    lower = pltpu.roll(upper, K, axis=1)
    work = jnp.concatenate(
        [
            jnp.where(lane < K, upper, jnp.where(lane == row + K, 1.0, 0.0)),
            jnp.where(lane < K, lower, jnp.where(lane == row + K + K // 2, 1.0, 0.0)),
        ],
        axis=0,
    )
    lane = lax.broadcasted_iota(jnp.int32, (K, LANES), 1)
    own = jnp.where(lane == lax.broadcasted_iota(jnp.int32, (K, LANES), 0), work, 0.0)
    column = 1.0 / jnp.sqrt(jnp.sum(own, axis=1, keepdims=True))
    line = jnp.where(lane[:1] < K, 1.0 / jnp.sqrt(jnp.sum(own, axis=0, keepdims=True)), 1.0)
    work = work * column * line
    count = K // 8
    parts = [work[8 * i : 8 * i + 8] for i in range(count)]
    sub = lax.broadcasted_iota(jnp.int32, (8, LANES), 0)
    diagonal = [jnp.ones((8, LANES), F32)] * count

    def full(value):
        return jnp.broadcast_to(value, (8, LANES))

    for j in range(0, K, 4):
        block, at = divmod(j, 8)
        own = parts[block]
        c1, c2, c3, c4 = [[full(parts[i][:, j + c : j + c + 1]) for i in range(block, count)] for c in range(4)]
        r1, r2, r3, r4 = [full(own[at + r : at + r + 1]) for r in range(4)]
        a11, a12, a13, a14 = [full(c[0][at : at + 1]) for c in (c1, c2, c3, c4)]
        a22, a23, a24 = [full(c[0][at + 1 : at + 2]) for c in (c2, c3, c4)]
        a33, a34 = [full(c[0][at + 2 : at + 3]) for c in (c3, c4)]
        a44 = full(c4[0][at + 3 : at + 4])
        first = a11 * a22 - a12 * a12
        scale = 1.0 / first
        l31, l32 = (a22 * a13 - a12 * a23) * scale, (a11 * a23 - a12 * a13) * scale
        l41, l42 = (a22 * a14 - a12 * a24) * scale, (a11 * a24 - a12 * a14) * scale
        s33 = a33 - (l31 * a13 + l32 * a23)
        s34 = a34 - (l31 * a14 + l32 * a24)
        s44 = a44 - (l41 * a14 + l42 * a24)
        r3 = r3 - (l31 * r1 + l32 * r2)
        r4 = r4 - (l41 * r1 + l42 * r2)
        second = s33 * s44 - s34 * s34
        again = 1.0 / second
        v1, v2 = (a22 * r1 - a12 * r2) * scale, (a11 * r2 - a12 * r1) * scale
        v3, v4 = (s44 * r3 - s34 * r4) * again, (s33 * r4 - s34 * r3) * again
        p1, p3 = 1.0 / a11, 1.0 / s33
        rows = (r2 - a12 * p1 * r1, r3, r4 - s34 * p3 * r3)
        diag = (a11, first * p1, s33, second * p3)
        for r in range(4):
            diagonal[block] = jnp.where(sub == at + r, diag[r], diagonal[block])
        for i in range(block, count):
            f1, f2, f3, f4 = [c[i - block] for c in (c1, c2, c3, c4)]
            f3 = f3 - (f1 * l31 + f2 * l32)
            f4 = f4 - (f1 * l41 + f2 * l42)
            new = parts[i] - ((f1 * v1 + f2 * v2) + (f3 * v3 + f4 * v4))
            if i == block:
                new = jnp.where(sub > at + 3, new, own)
                for r in range(3):
                    new = jnp.where(sub == at + 1 + r, rows[r], new)
            parts[i] = new
    parts = [part * (1.0 / jnp.sqrt(diag)) for part, diag in zip(parts, diagonal)]
    inverse_ref[...] = jnp.concatenate(parts, axis=0)[:, K:]


def inverse_of(gram):
    return pl.pallas_call(
        inverse_kernel,
        out_shape=jax.ShapeDtypeStruct((K, K), F32),
        in_specs=vmem(1),
        out_specs=vmem(1)[0],
        compiler_params=pltpu.CompilerParams(vmem_limit_bytes=8 * MIB),
        cost_estimate=pl.CostEstimate(flops=K**3 * 100, bytes_accessed=8 * K * K, transcendentals=K),
    )(gram)


def basis_kernel(scale, inverse_ref, s0, s3, s2, s1, basis_ref, sample):
    half = s0.shape[0]
    mine = own_quarter()
    for mask, ref in ((0, s0), (3, s3), (2, s2), (1, s1)):
        start = pl.multiple_of((mine ^ mask) * 2 * half, 2 * half)
        sample[pl.ds(start, half), :] = ref[:, :K]
        sample[pl.ds(start + half, half), :] = ref[:, K:]
    basis_ref[...] = lax.dot_general(
        inverse_ref[...] * scale,
        sample[...],
        (((1,), (1,)), ((), ())),
        precision=lax.Precision.HIGHEST,
        preferred_element_type=F32,
    )


def basis_of(inverse, quarters, rows, scale):
    return pl.pallas_call(
        functools.partial(basis_kernel, scale),
        out_shape=jax.ShapeDtypeStruct((K, rows), F32),
        in_specs=vmem(1 + len(quarters)),
        out_specs=vmem(1)[0],
        scratch_shapes=[VMEM((rows, K), F32)],
        compiler_params=pltpu.CompilerParams(vmem_limit_bytes=8 * MIB),
        cost_estimate=pl.CostEstimate(flops=12 * rows * K * K, bytes_accessed=8 * rows * K, transcendentals=0),
    )(inverse, *quarters)


def apply_kernel(first_group, inverse_ref, value_ref, *refs):
    out_ref, parts, sems = refs[-3:]
    high, low = split(inverse_ref[...])
    left = jnp.concatenate([high, low, high], axis=1)
    width = PER_GROUP * LANES
    copies = []
    for g in range(PER_GROUP):
        rows = [value_ref[pl.ds((g * PER_GROUP + t) * K, K), :] for t in range(PER_GROUP)]
        high, low = split(jnp.concatenate(rows, axis=1))
        right = jnp.concatenate([high, high, low], axis=0)
        parts[g] = jnp.dot(left, right, preferred_element_type=F32)
        at = pl.ds(pl.multiple_of(group_place(first_group + g) * width, width), width)
        copies.append(pltpu.make_async_copy(parts.at[g], out_ref.at[:, at], sems.at[g]))
        copies[g].start()
    for copy in copies:
        copy.wait()


def applied(first_group, inverse, value, begun=None):
    columns = BLOCKS * LANES
    more = [] if begun is None else [begun]
    return pl.pallas_call(
        functools.partial(apply_kernel, first_group),
        out_shape=jax.ShapeDtypeStruct((K, columns), F32),
        in_specs=vmem(2) + [pl.BlockSpec(memory_space=pl.ANY)] * len(more),
        out_specs=pl.BlockSpec(memory_space=pl.ANY),
        input_output_aliases={2: 0} if more else {},
        scratch_shapes=[VMEM((PER_GROUP, K, PER_GROUP * LANES), F32), pltpu.SemaphoreType.DMA((PER_GROUP,))],
        compiler_params=pltpu.CompilerParams(vmem_limit_bytes=8 * MIB),
        cost_estimate=pl.CostEstimate(flops=3 * columns * K * K, bytes_accessed=4 * columns * K, transcendentals=0),
    )(inverse, value, *more)


def along_col(value, mask):
    return lax.ppermute(value, "col", [(i, i ^ mask) for i in range(8)])


def along_row(value, masks):
    return lax.ppermute(value, "row", [(i, i ^ masks[i % 2]) for i in range(32)])


CORE = (1, 1)
FIRST = [(t << 3, t << 1) for t in range(4)]
SECOND = [(t << 1, t << 3) for t in range(4)]


def body(data_slab, sketch):
    rows = data_slab.shape[0]
    sent, sent_terms, kept, kept_terms = partial_samples(data_slab, sketch.T)
    got = [along_col(part, mask) for part, mask in zip(sent, SENT)]
    own = kept + got[0] + got[1] + got[2]
    own = own + along_col(own, 7)
    quarters = [own] + [along_col(own, mask) for mask in SENT]

    keep, send = terms_of(quarters, kept_terms, sent_terms)
    total = keep + along_row(send, CORE)
    size = PER_GROUP * K
    gram = total[4 * size :]
    places = {t: ORDER.index(t) * size for t in (3, 1, 2)}
    got = [along_row(jnp.concatenate([total[p : p + size], gram]), FIRST[t]) for t, p in places.items()]
    total = jnp.concatenate([total[:size], gram]) + got[0] + got[1] + got[2]
    got = [along_row(total, SECOND[t]) for t in (1, 3, 2)]
    total = total + got[0] + got[1] + got[2]

    inverse = inverse_of(total[size:])
    block = total[:size]
    mine = jnp.concatenate([block] + [along_row(block, FIRST[t]) for t in (1, 2, 3)])
    range_basis = basis_of(inverse, quarters, rows, math.sqrt(rows * lax.axis_size("row")))
    mine, inverse, range_basis = lax.optimization_barrier((mine, inverse, range_basis))
    theirs = along_row(mine, CORE)
    projected = applied(PER_GROUP, inverse, theirs, applied(0, inverse, mine))
    return range_basis.T, projected


def solution(mesh):
    placed = (P("row", "col"), P("col", None))
    return jax.shard_map(
        body,
        mesh=mesh,
        in_specs=placed,
        out_specs=(P("row", None), P(None, "col")),
        check_vma=False,
    )
```
